256 devices in a mesh: sta: 8 (over x, core), cel: 32 (over z, y).
Axes of the slice: x: 4, y: 4, z: 8, core: 2. Of those that a mesh axis runs over, the one named last changes fastest.
Arguments:
- model_vectors: bfloat16 [16, 262144], P('sta', 'cel'), may hold values from -6 to 6
- station_xyz: float32 [3, 262144], P(None, 'sta'), may hold values from 0 to 2, as said below
- cell_xyz: float32 [3, 262144], P(None, 'cel'), may hold values from -1 to 2, as said below
- weights: float32 [262144], P('sta'), may hold values from 0.25 to 4
- near_pairs: int32 [8, 32, 64, 2], P('sta', 'cel'), may hold values from 0 to 127, as said below
- near_count: int32 [8, 32], P('sta'), may hold values from 8 to 64, as said below
- mid_pairs: int32 [8, 32, 128, 2], P('sta', 'cel'), may hold values from 0 to 127, as said below
- mid_u: bfloat16 [8, 32, 128, 32, 256], P('sta', 'cel'), may hold values from -0.375 to 0.375
- mid_v: bfloat16 [8, 32, 128, 32, 256], P('sta', 'cel'), may hold values from -0.375 to 0.375
Outputs:
- predicted: float32 [16, 262144], P(None, ('sta', 'cel'))
- gradient: float32 [16, 262144], P('sta', 'cel')
The draws below stay inside these ranges and needn't reach their ends.
Inputs may be any that keep to these rules, and one draw needn't show every extreme that they name: `near_pairs`: entry 0 of a pair is a station tile below 128, entry 1 a cell tile below 32; a device's near and mid pairs are all different; slots at or past the device's near_count are ignored. `mid_pairs`: entry 0 a station tile below 128, entry 1 a cell tile below 32. `near_count`: each count is 64 divided by 1, 2, 4 or 8; some device has 64. `station_xyz`: east and north lie in 0 to 2; heights in 0.5 to 1. `cell_xyz`: east and north lie in 0 to 2; heights in -1 to -0.25.
All inputs are finite; a program needn't handle non-finite values.
Results may differ from the reference program's by a relative error of at most 0.015.
Values may be sent and summed in bfloat16 or wider, within the bound.
No kernel may reach another device: no remote copies, remote signals or barrier semaphores. Data moves between devices by JAX's collectives and lax.ppermute only.
A program may use at most 128 MiB of HBM per device.

```python
import math
import jax
import jax.numpy as jnp
from jax import lax

TILE = 256
RANK = 32
VECS = 16
ST_DEV = 128
CT_DEV = 32
NEAR_MAX = 64
MID_DEV = 128
NS = 262144
NC = 262144
N_STA = 8
N_CEL = 32


def block_lists(key):
    devices = N_STA * N_CEL
    subkeys = jax.random.split(key, devices)
    orders = jax.vmap(lambda subkey: jax.random.permutation(subkey, ST_DEV * CT_DEV))(subkeys)
    joined = jnp.stack([orders // CT_DEV, orders % CT_DEV], axis=-1).astype(jnp.int32)
    return joined.reshape(N_STA, N_CEL, ST_DEV * CT_DEV, 2)


def draw_near_pairs(key, part):
    shared = block_lists(key)
    return shared[:, :, :NEAR_MAX]


def draw_mid_pairs(key, part):
    shared = block_lists(key)
    return shared[:, :, NEAR_MAX:NEAR_MAX + MID_DEV]


def draw_near_count(key, part):
    key = jax.random.fold_in(key, 3)
    first_key, second_key = jax.random.split(key)
    devices = N_STA * N_CEL
    halvings = jax.random.randint(first_key, (devices,), 0, 4)
    chosen = jax.random.randint(second_key, (), 0, devices)
    halvings = jnp.where(jnp.arange(devices) == chosen, 0, halvings).astype(jnp.int32)
    counts = jnp.right_shift(jnp.full((devices,), NEAR_MAX, jnp.int32), halvings)
    return counts.reshape(N_STA, N_CEL).astype(jnp.int32)


def draw_station_xyz(key, part):
    key = jax.random.fold_in(key, 4)
    uniform_draw = jax.random.uniform(key, (3, NS), jnp.float32)
    return jnp.stack([2.0 * uniform_draw[0], 2.0 * uniform_draw[1], 0.5 + 0.5 * uniform_draw[2]]).astype(jnp.float32)


def draw_cell_xyz(key, part):
    key = jax.random.fold_in(key, 5)
    uniform_draw = jax.random.uniform(key, (3, NC), jnp.float32)
    return jnp.stack([2.0 * uniform_draw[0], 2.0 * uniform_draw[1], -1.0 + 0.75 * uniform_draw[2]]).astype(jnp.float32)


def block_levels(stream_key, shape, pieces, low, top_value):
    gain = 1.0
    for position, shards_of in pieces:
        draws = jax.random.uniform(jax.random.fold_in(jax.random.fold_in(stream_key, 6), position), (shards_of,), jnp.float32, low / len(pieces), top_value / len(pieces))
        gain = gain * jnp.repeat(jnp.exp(draws), shape[position] // shards_of).reshape((-1,) + (1,) * (len(shape) - 1 - position))
    return gain


def centred(rng, extent, width, reach, shards=(), held_as=jnp.bfloat16):
    gain = block_levels(rng, extent, shards, -0.22, 0.18) if shards else 1.0
    drawn = jax.random.normal(rng, extent, jnp.float32) * width * gain
    return jnp.minimum(jnp.maximum(drawn, -reach), reach).astype(held_as)


def setup_inputs(seed: int = 0) -> dict:
    key_list = jax.random.split(jax.random.key(seed), 10)
    model_vectors = centred(key_list[0], (VECS, NC), 1.0, 6.0, ((0, 8), (1, 32)))
    station_xyz = draw_station_xyz(jax.random.fold_in(key_list[9], 71), 0)
    cell_xyz = draw_cell_xyz(jax.random.fold_in(key_list[9], 71), 0)
    weights = jnp.clip(jnp.exp(math.log(4.0) - 2.7725887 * jax.random.uniform(key_list[3], (NS,), jnp.float32) ** block_levels(key_list[3], (NS,), ((0, 8),), -0.2, 0.2)), 0.25, 4.0)
    near_pairs = draw_near_pairs(jax.random.fold_in(key_list[9], 71), 0)
    near_count = draw_near_count(jax.random.fold_in(key_list[9], 71), 0)
    mid_pairs = draw_mid_pairs(jax.random.fold_in(key_list[9], 71), 0)
    mid_u = centred(key_list[7], (N_STA, N_CEL, MID_DEV, RANK, TILE), (RANK * 8) ** -0.5, 0.375, ((0, 8), (1, 32)))
    mid_v = centred(key_list[8], (N_STA, N_CEL, MID_DEV, RANK, TILE), TILE ** -0.5, 0.375, ((0, 8), (1, 32)))
    return dict(model_vectors=model_vectors, station_xyz=station_xyz, cell_xyz=cell_xyz, weights=weights, near_pairs=near_pairs, near_count=near_count, mid_pairs=mid_pairs, mid_u=mid_u, mid_v=mid_v)


VOLUME = 0.03125
FIELD_X = 0.17101
FIELD_Y = 0.46985
FIELD_Z = -0.86603

def kernel_tile(stations, cell_points):
    delta_x = stations[0][None, :] - cell_points[0][:, None]
    delta_y = stations[1][None, :] - cell_points[1][:, None]
    delta_z = stations[2][None, :] - cell_points[2][:, None]
    inverse = lax.rsqrt(delta_x * delta_x + delta_y * delta_y + delta_z * delta_z)
    aligned = (FIELD_X * delta_x + FIELD_Y * delta_y + FIELD_Z * delta_z) * inverse
    return VOLUME * (3.0 * aligned * aligned - 1.0) * inverse * inverse * inverse

def global_lists(pairs, sta_count, cel_count):
    devices = N_STA * N_CEL
    slot_total = pairs.shape[2]
    device_index = jnp.arange(devices, dtype=jnp.int32)
    flat_pairs = pairs.reshape(devices, slot_total, 2).astype(jnp.int32)
    tile_rows = device_index[:, None] // N_CEL * sta_count + flat_pairs[:, :, 0]
    columns = device_index[:, None] % N_CEL * cel_count + flat_pairs[:, :, 1]
    return (tile_rows.reshape(-1).astype(jnp.int32), columns.reshape(-1).astype(jnp.int32))

def reference(model_vectors, station_xyz, cell_xyz, weights, near_pairs, near_count, mid_pairs, mid_u, mid_v):
    station_grid = station_xyz.reshape(3, NS // TILE, TILE)
    cell_grid = cell_xyz.reshape(3, NC // TILE, TILE)
    vector_tiles = model_vectors.reshape(VECS, NC // TILE, TILE)
    near_rows, near_columns = global_lists(near_pairs, ST_DEV, CT_DEV)
    live_slots = (jnp.arange(NEAR_MAX, dtype=jnp.int32)[None, :] < near_count.reshape(N_STA * N_CEL, 1).astype(jnp.int32)).reshape(-1)
    mid_rows, mid_columns = global_lists(mid_pairs, ST_DEV, CT_DEV)
    u_factor = mid_u.reshape(-1, RANK, TILE).astype(jnp.float32)
    v_factor = mid_v.reshape(-1, RANK, TILE).astype(jnp.float32)

    def near_block(row_index, column_index):
        return kernel_tile(station_grid[:, row_index], cell_grid[:, column_index]).astype(jnp.bfloat16)
    picked = vector_tiles[:, mid_columns].astype(jnp.float32)
    reduced = lax.optimization_barrier(jnp.einsum('vmc,mrc->vmr', picked, v_factor).astype(jnp.bfloat16)).astype(jnp.float32)
    spread = jnp.einsum('vmr,mrs->vms', reduced, u_factor)
    forward_sum = jnp.zeros((VECS, NS // TILE, TILE), jnp.float32).at[:, mid_rows].add(spread)

    def forward_step(totals, slot_item):
        row_index, column_index, is_live = slot_item
        contribution = jnp.dot(vector_tiles[:, column_index], near_block(row_index, column_index), preferred_element_type=jnp.float32)
        return (totals.at[:, row_index].add(jnp.where(is_live, contribution, 0.0)), None)
    forward_sum = lax.scan(forward_step, forward_sum, (near_rows, near_columns, live_slots))[0]
    predicted = forward_sum.reshape(VECS, NS)
    weighted = (predicted * weights[None, :]).astype(jnp.bfloat16)
    data_tiles = weighted.reshape(VECS, NS // TILE, TILE)
    gathered = data_tiles[:, mid_rows].astype(jnp.float32)
    pulled = lax.optimization_barrier(jnp.einsum('vms,mrs->vmr', gathered, u_factor).astype(jnp.bfloat16)).astype(jnp.float32)
    expanded = jnp.einsum('vmr,mrc->vmc', pulled, v_factor)
    adjoint_sum = jnp.zeros((VECS, NC // TILE, TILE), jnp.float32).at[:, mid_columns].add(expanded)

    def adjoint_step(totals, slot_item):
        row_index, column_index, is_live = slot_item
        contribution = jnp.dot(data_tiles[:, row_index], near_block(row_index, column_index).T, preferred_element_type=jnp.float32)
        return (totals.at[:, column_index].add(jnp.where(is_live, contribution, 0.0)), None)
    adjoint_sum = lax.scan(adjoint_step, adjoint_sum, (near_rows, near_columns, live_slots))[0]
    return (predicted, adjoint_sum.reshape(VECS, NC))
```

```python
import functools

import jax
import jax.numpy as jnp
from jax import lax
from jax.experimental import pallas as pl
from jax.experimental.pallas import tpu as pltpu
from jax.sharding import PartitionSpec as P

VOLUME = 0.03125
FIELD = (0.17101, 0.46985, -0.86603)
ROOT = (3.0 * VOLUME) ** 0.5

TILE = 256
VECS = 16
GROUP = 8
MIB = 1 << 20
F32 = jnp.float32
BF16 = jnp.bfloat16

SMEM = pl.BlockSpec(memory_space=pltpu.SMEM)
VMEM = pl.BlockSpec(memory_space=pltpu.VMEM)
ANY = pl.BlockSpec(memory_space=pl.ANY)


def split3(x):
    high = x.astype(BF16).astype(F32)
    rest = x - high
    middle = rest.astype(BF16).astype(F32)
    return high, middle, rest - middle


def near_kernel(meta, pairs, stations, cells, out, station_rows, cell_rows):
    step = pl.program_id(0)
    count = meta[0]

    @pl.when(step == 0)
    def _():
        def station_chunk(i, carry):
            at = pl.ds(pl.multiple_of(i * 2048, 2048), 2048)
            x, y, z = (stations[d : d + 1, at] for d in range(3))
            station_rows[0:1, at] = x
            station_rows[1:2, at] = y
            station_rows[2:3, at] = z
            station_rows[3:4, at] = x * x + y * y + z * z
            station_rows[4:5, at] = ROOT * (FIELD[0] * x + FIELD[1] * y + FIELD[2] * z)
            station_rows[5:6, at] = jnp.ones_like(x)
            station_rows[6:8, at] = jnp.zeros((2, 2048), F32)
            return carry

        lax.fori_loop(0, stations.shape[1] // 2048, station_chunk, 0)

        def cell_chunk(i, carry):
            at = pl.ds(pl.multiple_of(i * TILE, TILE), TILE)
            x, y, z = (cells[d : d + 1, at] for d in range(3))
            zero = jnp.zeros_like(x)
            one = jnp.ones_like(x)
            square = x * x + y * y + z * z
            along = -ROOT * (FIELD[0] * x + FIELD[1] * y + FIELD[2] * z)
            lines = lax.broadcasted_iota(jnp.int32, (8, TILE), 0)

            def stack(values):
                total = jnp.zeros((8, TILE), F32)
                for line, value in values:
                    total = jnp.where(lines == line, value, total)
                return total

            wide = stack(((0, -2.0 * x), (1, -2.0 * y), (2, -2.0 * z), (3, one), (5, square)))
            flat = stack(((4, one), (5, along)))
            for position, block in enumerate((wide, flat)):
                h, m, l = split3(block)
                turned = jnp.concatenate((h, h, h, m, m, l), axis=0).T
                cell_rows[i, position * TILE : (position + 1) * TILE, :] = turned.astype(BF16)
            return carry

        lax.fori_loop(0, cells.shape[1] // TILE, cell_chunk, 0)

    @pl.when(step * GROUP < count)
    def _():
        for j in range(GROUP):
            row = pairs[0, step * GROUP + j]
            column = pairs[1, step * GROUP + j]
            at = pl.ds(pl.multiple_of(row * TILE, TILE), TILE)
            h, m, l = split3(station_rows[:, at])
            right = jnp.concatenate((h, m, l, h, m, h), axis=0).astype(BF16)
            both = jnp.dot(cell_rows[column], right, preferred_element_type=F32)
            distance, along = both[:TILE], both[TILE:]
            inverse = lax.rsqrt(distance)
            square = inverse * inverse
            out[j] = ((along * along * square - VOLUME) * (square * inverse)).astype(BF16)


def block_mask():
    lines = lax.broadcasted_iota(jnp.int32, (GROUP * VECS, TILE), 0) // VECS
    lanes = lax.broadcasted_iota(jnp.int32, (GROUP * VECS, TILE), 1) // (TILE // GROUP)
    return lines == lanes


def fetch_blocks(blocks, held, sem, groups):
    def start(g, carry):
        at = pl.ds(g * GROUP, GROUP)
        pltpu.make_async_copy(blocks.at[at], held.at[at], sem.at[g]).start()
        return carry

    lax.fori_loop(0, groups, start, 0)


def await_group(blocks, held, sem, g):
    at = pl.ds(g * GROUP, GROUP)
    pltpu.make_async_copy(blocks.at[at], held.at[at], sem.at[g]).wait()


def contract(a, b, dim):
    return lax.dot_general(a, b, (((1,), (dim,)), ((), ())), preferred_element_type=F32)


def lanes_of(column):
    return pl.ds(pl.multiple_of(column * TILE, TILE), TILE)


def place(meta, row):
    share = row >> 2
    slot = ((share & 3) ^ meta[1]) * 8 + ((share >> 2) ^ meta[2])
    return slot, lanes_of(row & 3)


def forward_kernel(meta, near, mid, *refs):
    parts = refs[:8]
    u_ref, v_ref, blocks = refs[8:11]
    outs = refs[11:15]
    stacked, vectors, total, held, sem = refs[15:]
    groups = meta[0] // GROUP
    fetch_blocks(blocks, held, sem, groups)
    for k in range(8):
        stacked[2 * k : 2 * k + 2, :] = parts[k][...].astype(F32)
    vectors[...] = stacked[...].astype(BF16)
    total[...] = jnp.zeros_like(total)
    mask = block_mask()

    def mid_step(i, carry):
        sums = []
        for q in range(4):
            g = i * 4 + q
            source = jnp.concatenate(
                [vectors[:, lanes_of(mid[1, g * GROUP + j])] for j in range(GROUP)], axis=0
            )
            reduced = contract(source, v_ref[g], 1)
            reduced = jnp.where(mask, reduced, 0.0).astype(BF16)
            sums.append(contract(reduced, u_ref[g], 0))
        for q in range(4):
            for j in range(GROUP):
                slot, lanes = place(meta, mid[0, (i * 4 + q) * GROUP + j])
                total[slot, :, lanes] += sums[q][j * VECS : (j + 1) * VECS]
        return carry

    lax.fori_loop(0, u_ref.shape[0] // 4, mid_step, 0)

    def near_step(g, carry):
        await_group(blocks, held, sem, g)
        sums = [
            contract(vectors[:, lanes_of(near[1, g * GROUP + j])], held[g * GROUP + j], 0)
            for j in range(GROUP)
        ]
        for j in range(GROUP):
            slot, lanes = place(meta, near[0, g * GROUP + j])
            total[slot, :, lanes] += sums[j]
        return carry

    lax.fori_loop(0, groups, near_step, 0)
    for j in range(4):
        outs[j][...] = total[8 * j : 8 * j + 8].astype(outs[j].dtype)


def row_sum_kernel(own, a, b, c, *outs):
    for k in range(8):
        total = own[k] + a[k].astype(F32) + b[k].astype(F32) + c[k].astype(F32)
        outs[k][...] = total.astype(outs[k].dtype)


def weigh_kernel(meta, own, *refs):
    parts = refs[:7]
    weights, predicted, weighted = refs[7:10]
    total = own[...]
    for part in parts:
        total = total + part[...].astype(F32)
    share = weights[pl.ds(pl.multiple_of(meta[3] * 8, 8), 8), :]
    for r in range(8):
        at = slice(r * 128, (r + 1) * 128)
        weighted[:, at] = (total[:, at] * share[r : r + 1, :]).astype(BF16)
    for place_of in range(8):

        @pl.when(meta[4] == place_of)
        def _():
            for k in range(8):
                line = 2 * (k ^ place_of)
                predicted[line : line + 2, :] = total[2 * k : 2 * k + 2]


def join_kernel(*refs):
    for k in range(8):
        refs[8][k] = refs[k][...]


def adjoint_kernel(meta, near, mid, *refs):
    pieces = refs[:4]
    u_ref, v_ref, blocks = refs[4:7]
    outs = refs[7:15]
    data, total, held, sem = refs[15:]
    groups = meta[0] // GROUP
    fetch_blocks(blocks, held, sem, groups)
    for j in range(4):
        data[8 * j : 8 * j + 8] = pieces[j][...]
    total[...] = jnp.zeros_like(total)
    mask = block_mask()

    def station_tile(row):
        slot, lanes = place(meta, row)
        return data[slot, :, lanes]

    def mid_step(i, carry):
        sums = []
        for q in range(4):
            g = i * 4 + q
            source = jnp.concatenate(
                [station_tile(mid[0, g * GROUP + j]) for j in range(GROUP)], axis=0
            )
            pulled = contract(source, u_ref[g], 1)
            pulled = jnp.where(mask, pulled, 0.0).astype(BF16)
            sums.append(contract(pulled, v_ref[g], 0))
        for q in range(4):
            for j in range(GROUP):
                lanes = lanes_of(mid[1, (i * 4 + q) * GROUP + j])
                total[:, lanes] += sums[q][j * VECS : (j + 1) * VECS]
        return carry

    lax.fori_loop(0, u_ref.shape[0] // 4, mid_step, 0)

    def near_step(g, carry):
        await_group(blocks, held, sem, g)
        sums = [
            contract(station_tile(near[0, g * GROUP + j]), held[g * GROUP + j], 1)
            for j in range(GROUP)
        ]
        for j in range(GROUP):
            total[:, lanes_of(near[1, g * GROUP + j])] += sums[j]
        return carry

    lax.fori_loop(0, groups, near_step, 0)
    for k in range(8):
        outs[k][...] = total[2 * k : 2 * k + 2, :].astype(outs[k].dtype)


def params(mib):
    return pltpu.CompilerParams(vmem_limit_bytes=mib * MIB)


def body(
    model_vectors, station_xyz, cell_xyz, weights, near_pairs, near_count, mid_pairs, mid_u, mid_v
):
    sta_index = lax.axis_index("sta")
    cel_index = lax.axis_index("cel")
    slots = near_pairs.shape[2]
    z_index = cel_index // 4
    y_index = cel_index % 4
    own_count = near_count[0, cel_index]
    meta = jnp.stack([own_count, y_index, z_index, cel_index, sta_index]).astype(jnp.int32)
    near = near_pairs[0, 0].T
    mid = mid_pairs[0, 0].T
    u_factor = mid_u.reshape(-1, TILE, TILE)
    v_factor = mid_v.reshape(-1, TILE, TILE)

    def over_sta(x, k):
        return lax.ppermute(x, "sta", [(i, i ^ k) for i in range(8)])

    def over_y(x, j):
        return lax.ppermute(x, "cel", [(i, i ^ j) for i in range(32)])

    def over_z(x, k):
        return lax.ppermute(x, "cel", [(i, i ^ (4 * k)) for i in range(32)])

    vector_parts = [model_vectors] + [over_sta(model_vectors, k) for k in range(1, 8)]

    blocks = pl.pallas_call(
        near_kernel,
        grid_spec=pltpu.PrefetchScalarGridSpec(
            num_scalar_prefetch=2,
            grid=(slots // GROUP,),
            in_specs=[
                pl.BlockSpec(station_xyz.shape, lambda i, meta, pairs: (0, 0)),
                pl.BlockSpec(cell_xyz.shape, lambda i, meta, pairs: (0, 0)),
            ],
            out_specs=pl.BlockSpec(
                (GROUP, TILE, TILE),
                lambda i, meta, pairs: (jnp.minimum(i, meta[0] // GROUP - 1), 0, 0),
            ),
            scratch_shapes=[
                pltpu.VMEM((8, station_xyz.shape[1]), F32),
                pltpu.VMEM((cell_xyz.shape[1] // TILE, 2 * TILE, 48), BF16),
            ],
        ),
        out_shape=jax.ShapeDtypeStruct((slots, TILE, TILE), BF16),
        compiler_params=params(24),
        cost_estimate=pl.CostEstimate(
            flops=slots * 2 * 512 * 48 * 256, bytes_accessed=10 * MIB, transcendentals=slots * 65536
        ),
        name="near_blocks",
    )(meta, near, station_xyz, cell_xyz)

    wide = jax.ShapeDtypeStruct((8, VECS, 1024), BF16)
    shares = pl.pallas_call(
        forward_kernel,
        in_specs=[SMEM] * 3 + [VMEM] * 10 + [ANY],
        out_specs=[VMEM] * 4,
        out_shape=[jax.ShapeDtypeStruct(wide.shape, F32)] + [wide] * 3,
        scratch_shapes=[
            pltpu.VMEM((VECS, 8192), F32),
            pltpu.VMEM((VECS, 8192), BF16),
            pltpu.VMEM((32, VECS, 1024), F32),
            pltpu.VMEM((slots, TILE, TILE), BF16),
            pltpu.SemaphoreType.DMA((slots // GROUP,)),
        ],
        compiler_params=params(32),
        name="forward",
    )(meta, near, mid, *vector_parts, u_factor, v_factor, blocks)

    from_y = [over_y(shares[j], j) for j in range(1, 4)]
    narrow = jax.ShapeDtypeStruct((VECS, 1024), BF16)
    sums = pl.pallas_call(
        row_sum_kernel,
        in_specs=[VMEM] * 4,
        out_specs=[VMEM] * 8,
        out_shape=[jax.ShapeDtypeStruct(narrow.shape, F32)] + [narrow] * 7,
        compiler_params=params(8),
        name="row_sum",
    )(shares[0], *from_y)
    from_z = [over_z(sums[k], k) for k in range(1, 8)]
    predicted, weighted = pl.pallas_call(
        weigh_kernel,
        in_specs=[SMEM] + [VMEM] * 9,
        out_specs=[VMEM] * 2,
        out_shape=[jax.ShapeDtypeStruct(narrow.shape, F32), narrow],
        compiler_params=params(4),
        name="weigh",
    )(meta, sums[0], *from_z, weights.reshape(-1, 128))

    gathered = [weighted] + [over_z(weighted, k) for k in range(1, 8)]
    column = pl.pallas_call(
        join_kernel,
        in_specs=[VMEM] * 8,
        out_specs=VMEM,
        out_shape=wide,
        compiler_params=params(4),
        name="join",
    )(*gathered)
    columns = [column] + [over_y(column, j) for j in range(1, 4)]

    pair = jax.ShapeDtypeStruct((2, 8192), BF16)
    terms = pl.pallas_call(
        adjoint_kernel,
        in_specs=[SMEM] * 3 + [VMEM] * 6 + [ANY],
        out_specs=[VMEM] * 8,
        out_shape=[jax.ShapeDtypeStruct(pair.shape, F32)] + [pair] * 7,
        scratch_shapes=[
            pltpu.VMEM((32, VECS, 1024), BF16),
            pltpu.VMEM((VECS, 8192), F32),
            pltpu.VMEM((slots, TILE, TILE), BF16),
            pltpu.SemaphoreType.DMA((slots // GROUP,)),
        ],
        compiler_params=params(32),
        name="adjoint",
    )(meta, near, mid, *columns, u_factor, v_factor, blocks)
    gradient = terms[0]
    for k in range(1, 8):
        gradient = gradient + over_sta(terms[k], k).astype(F32)
    return (predicted, gradient)


def solution(mesh):
    return jax.shard_map(
        body,
        mesh=mesh,
        in_specs=(
            P("sta", "cel"),
            P(None, "sta"),
            P(None, "cel"),
            P("sta"),
            P("sta", "cel", None, None),
            P("sta", None),
            P("sta", "cel", None, None),
            P("sta", "cel", None, None, None),
            P("sta", "cel", None, None, None),
        ),
        out_specs=(P(None, ("sta", "cel")), P("sta", "cel")),
        check_vma=False,
    )
```

```python
import functools

import jax
import jax.numpy as jnp
from jax import lax
from jax.experimental import pallas as pl
from jax.experimental.pallas import tpu as pltpu
from jax.sharding import PartitionSpec as P

VOLUME = 0.03125
FIELD = (0.17101, 0.46985, -0.86603)
ROOT = (3.0 * VOLUME) ** 0.5

TILE = 256
VECS = 16
GROUP = 8
MIB = 1 << 20
WIDE = 8
TALL = 4
F32 = jnp.float32
BF16 = jnp.bfloat16

SMEM = pl.BlockSpec(memory_space=pltpu.SMEM)
VMEM = pl.BlockSpec(memory_space=pltpu.VMEM)
ANY = pl.BlockSpec(memory_space=pl.ANY)


def split3(x):
    high = x.astype(BF16).astype(F32)
    rest = x - high
    middle = rest.astype(BF16).astype(F32)
    return high, middle, rest - middle


def near_kernel(counts, pairs, stations, cells, out, station_rows, cell_rows):
    def station_chunk(i, carry):
        at = pl.ds(pl.multiple_of(i * 2048, 2048), 2048)
        x, y, z = (stations[d : d + 1, at] for d in range(3))
        station_rows[0:1, at] = x
        station_rows[1:2, at] = y
        station_rows[2:3, at] = z
        station_rows[3:4, at] = x * x + y * y + z * z
        station_rows[4:5, at] = ROOT * (FIELD[0] * x + FIELD[1] * y + FIELD[2] * z)
        station_rows[5:6, at] = jnp.ones_like(x)
        station_rows[6:8, at] = jnp.zeros((2, 2048), F32)
        return carry

    lax.fori_loop(0, stations.shape[1] // 2048, station_chunk, 0)

    def cell_chunk(i, carry):
        at = pl.ds(pl.multiple_of(i * TILE, TILE), TILE)
        x, y, z = (cells[d : d + 1, at] for d in range(3))
        zero = jnp.zeros_like(x)
        one = jnp.ones_like(x)
        square = x * x + y * y + z * z
        along = -ROOT * (FIELD[0] * x + FIELD[1] * y + FIELD[2] * z)
        lines = lax.broadcasted_iota(jnp.int32, (8, TILE), 0)

        def stack(values):
            total = jnp.zeros((8, TILE), F32)
            for line, value in values:
                total = jnp.where(lines == line, value, total)
            return total

        wide = stack(((0, -2.0 * x), (1, -2.0 * y), (2, -2.0 * z), (3, one), (5, square)))
        flat = stack(((4, one), (5, along)))
        for position, block in enumerate((wide, flat)):
            h, m, l = split3(block)
            turned = jnp.concatenate((h, h, h, m, m, l), axis=0).T
            cell_rows[i, position * TILE : (position + 1) * TILE, :] = turned.astype(BF16)
        return carry

    lax.fori_loop(0, cells.shape[1] // TILE, cell_chunk, 0)

    def step_blocks(step, carry):
        for j in range(GROUP):
            row = pairs[0, step * GROUP + j]
            column = pairs[1, step * GROUP + j]
            at = pl.ds(pl.multiple_of(row * TILE, TILE), TILE)
            h, m, l = split3(station_rows[:, at])
            right = jnp.concatenate((h, m, l, h, m, h), axis=0).astype(BF16)
            both = jnp.dot(cell_rows[column], right, preferred_element_type=F32)
            distance, along = both[:TILE], both[TILE:]
            inverse = lax.rsqrt(distance)
            square = inverse * inverse
            out[step * GROUP + j] = ((along * along * square - VOLUME) * (square * inverse)).astype(BF16)
        return carry

    lax.fori_loop(0, near_groups(counts), step_blocks, 0)


def block_mask():
    lines = lax.broadcasted_iota(jnp.int32, (GROUP * VECS, TILE), 0) // VECS
    lanes = lax.broadcasted_iota(jnp.int32, (GROUP * VECS, TILE), 1) // (TILE // GROUP)
    return lines == lanes


def near_groups(counts):
    return counts[0, lax.axis_index("cel")] // GROUP


def contract(a, b, dim):
    return lax.dot_general(a, b, (((1,), (dim,)), ((), ())), preferred_element_type=F32)


def lanes_of(column):
    return pl.ds(pl.multiple_of(column * TILE, TILE), TILE)


def place(cel, row):
    share = (row >> 2) ^ cel
    return (share & (WIDE - 1)) * TALL + (share >> 3), lanes_of(row & 3)


def forward_kernel(counts, near, mid, *refs):
    parts = refs[:4]
    u_ref, v_ref, blocks = refs[4:7]
    outs = refs[7:15]
    stacked, vectors, total = refs[15:]
    cel = lax.axis_index("cel")
    for k in range(4):
        stacked[4 * k : 4 * k + 4, :] = parts[k][...].astype(F32)
    vectors[...] = stacked[...].astype(BF16)
    total[...] = jnp.zeros_like(total)
    mask = block_mask()

    def mid_step(i, carry):
        sums = []
        for q in range(4):
            g = i * 4 + q
            source = jnp.concatenate(
                [vectors[:, lanes_of(mid[1, g * GROUP + j])] for j in range(GROUP)], axis=0
            )
            reduced = contract(source, v_ref[g], 1)
            reduced = jnp.where(mask, reduced, 0.0).astype(BF16)
            sums.append(contract(reduced, u_ref[g], 0))
        for q in range(4):
            for j in range(GROUP):
                slot, lanes = place(cel, mid[0, (i * 4 + q) * GROUP + j])
                total[slot, :, lanes] += sums[q][j * VECS : (j + 1) * VECS]
        return carry

    lax.fori_loop(0, u_ref.shape[0] // 4, mid_step, 0)

    def near_step(g, carry):
        sums = [
            contract(vectors[:, lanes_of(near[1, g * GROUP + j])], blocks[g * GROUP + j], 0)
            for j in range(GROUP)
        ]
        for j in range(GROUP):
            slot, lanes = place(cel, near[0, g * GROUP + j])
            total[slot, :, lanes] += sums[j]
        return carry

    lax.fori_loop(0, near_groups(counts), near_step, 0)
    for i in range(WIDE):
        outs[i][...] = total[TALL * i : TALL * (i + 1)].astype(outs[i].dtype)


def share_sum_kernel(own, *refs):
    parts, outs = refs[: WIDE - 1], refs[WIDE - 1 :]
    for k in range(TALL):
        total = own[k]
        for part in parts:
            total = total + part[k].astype(F32)
        outs[k][...] = total.astype(outs[k].dtype)


def weigh_kernel(own, *refs):
    parts = refs[: TALL - 1]
    weights, predicted, weighted = refs[TALL - 1 :]
    sta, cel = lax.axis_index("sta"), lax.axis_index("cel")
    total = own[...]
    for part in parts:
        total = total + part[...].astype(F32)
    share = weights[pl.ds(pl.multiple_of(cel * 8, 8), 8), :]
    for r in range(8):
        at = slice(r * 128, (r + 1) * 128)
        weighted[:, at] = (total[:, at] * share[r : r + 1, :]).astype(BF16)
    for place_of in range(8):

        @pl.when(sta == place_of)
        def _():
            for k in range(8):
                line = 2 * (k ^ place_of)
                predicted[line : line + 2, :] = total[2 * k : 2 * k + 2]


def join_kernel(*refs):
    for k in range(TALL):
        refs[TALL][k] = refs[k][...]


def adjoint_kernel(counts, near, mid, *refs):
    pieces = refs[:WIDE]
    u_ref, v_ref, blocks, kept, swapped, data, total = refs[WIDE:]
    cel = lax.axis_index("cel")
    for i in range(WIDE):
        data[TALL * i : TALL * (i + 1)] = pieces[i][...]
    total[...] = jnp.zeros_like(total)
    mask = block_mask()

    def station_tile(row):
        slot, lanes = place(cel, row)
        return data[slot, :, lanes]

    def mid_step(i, carry):
        sums = []
        for q in range(4):
            g = i * 4 + q
            source = jnp.concatenate(
                [station_tile(mid[0, g * GROUP + j]) for j in range(GROUP)], axis=0
            )
            pulled = contract(source, u_ref[g], 1)
            pulled = jnp.where(mask, pulled, 0.0).astype(BF16)
            sums.append(contract(pulled, v_ref[g], 0))
        for q in range(4):
            for j in range(GROUP):
                lanes = lanes_of(mid[1, (i * 4 + q) * GROUP + j])
                total[:, lanes] += sums[q][j * VECS : (j + 1) * VECS]
        return carry

    lax.fori_loop(0, u_ref.shape[0] // 4, mid_step, 0)

    def near_step(g, carry):
        sums = [
            contract(station_tile(near[0, g * GROUP + j]), blocks[g * GROUP + j], 1)
            for j in range(GROUP)
        ]
        for j in range(GROUP):
            total[:, lanes_of(near[1, g * GROUP + j])] += sums[j]
        return carry

    lax.fori_loop(0, near_groups(counts), near_step, 0)
    for t in range(4):
        kept[2 * t : 2 * t + 2, :] = total[4 * t : 4 * t + 2, :]
    swapped[...] = jnp.concatenate(
        [total[4 * t + 2 : 4 * t + 4, :] for t in range(4)], axis=0
    ).astype(BF16)


def chip_sum_kernel(kept, swapped, *outs):
    total = kept[...] + swapped[...].astype(F32)
    for t in range(4):
        outs[t][...] = total[2 * t : 2 * t + 2].astype(outs[t].dtype)


def params(mib):
    return pltpu.CompilerParams(vmem_limit_bytes=mib * MIB)


def body(
    model_vectors, station_xyz, cell_xyz, weights, near_pairs, near_count, mid_pairs, mid_u, mid_v
):
    slots = near_pairs.shape[2]
    near = near_pairs[0, 0].T
    mid = mid_pairs[0, 0].T
    u_factor = mid_u.reshape(-1, TILE, TILE)
    v_factor = mid_v.reshape(-1, TILE, TILE)

    def over_sta(x, k):
        return lax.ppermute(x, "sta", [(i, i ^ k) for i in range(8)])

    def over_cel(x, k):
        return lax.ppermute(x, "cel", [(i, i ^ k) for i in range(32)])

    chip_vectors = jnp.concatenate((model_vectors, over_sta(model_vectors, 1)), axis=0)
    vector_parts = [chip_vectors] + [over_sta(chip_vectors, 2 * k) for k in range(1, 4)]

    blocks = pl.pallas_call(
        near_kernel,
        in_specs=[SMEM] * 2 + [VMEM] * 2,
        out_specs=VMEM,
        out_shape=jax.ShapeDtypeStruct((slots, TILE, TILE), BF16),
        scratch_shapes=[
            pltpu.VMEM((8, station_xyz.shape[1]), F32),
            pltpu.VMEM((cell_xyz.shape[1] // TILE, 2 * TILE, 48), BF16),
        ],
        compiler_params=params(24),
        cost_estimate=pl.CostEstimate(
            flops=slots * 2 * 512 * 48 * 256, bytes_accessed=10 * MIB, transcendentals=slots * 65536
        ),
        name="near_blocks",
    )(near_count, near, station_xyz, cell_xyz)

    wide = jax.ShapeDtypeStruct((TALL, VECS, 1024), BF16)
    shares = pl.pallas_call(
        forward_kernel,
        in_specs=[SMEM] * 3 + [VMEM] * 7,
        out_specs=[VMEM] * WIDE,
        out_shape=[jax.ShapeDtypeStruct(wide.shape, F32)] + [wide] * (WIDE - 1),
        scratch_shapes=[
            pltpu.VMEM((VECS, 8192), F32),
            pltpu.VMEM((VECS, 8192), BF16),
            pltpu.VMEM((32, VECS, 1024), F32),
        ],
        compiler_params=params(24),
        name="forward",
    )(near_count, near, mid, *vector_parts, u_factor, v_factor, blocks)

    from_wide = [over_cel(shares[i], i) for i in range(1, WIDE)]
    narrow = jax.ShapeDtypeStruct((VECS, 1024), BF16)
    sums = pl.pallas_call(
        share_sum_kernel,
        in_specs=[VMEM] * WIDE,
        out_specs=[VMEM] * TALL,
        out_shape=[jax.ShapeDtypeStruct(narrow.shape, F32)] + [narrow] * (TALL - 1),
        compiler_params=params(8),
        name="share_sum",
    )(shares[0], *from_wide)
    from_tall = [over_cel(sums[k], WIDE * k) for k in range(1, TALL)]
    predicted, weighted = pl.pallas_call(
        weigh_kernel,
        in_specs=[VMEM] * (TALL + 1),
        out_specs=[VMEM] * 2,
        out_shape=[jax.ShapeDtypeStruct(narrow.shape, F32), narrow],
        compiler_params=params(4),
        name="weigh",
    )(sums[0], *from_tall, weights.reshape(-1, 128))

    gathered = [weighted] + [over_cel(weighted, WIDE * k) for k in range(1, TALL)]
    column = pl.pallas_call(
        join_kernel,
        in_specs=[VMEM] * TALL,
        out_specs=VMEM,
        out_shape=wide,
        compiler_params=params(4),
        name="join",
    )(*gathered)
    columns = [column] + [over_cel(column, i) for i in range(1, WIDE)]

    lines = jax.ShapeDtypeStruct((8, 8192), BF16)
    kept, swapped = pl.pallas_call(
        adjoint_kernel,
        in_specs=[SMEM] * 3 + [VMEM] * (WIDE + 3),
        out_specs=[VMEM] * 2,
        out_shape=[jax.ShapeDtypeStruct(lines.shape, F32), lines],
        scratch_shapes=[
            pltpu.VMEM((32, VECS, 1024), BF16),
            pltpu.VMEM((VECS, 8192), F32),
        ],
        compiler_params=params(24),
        name="adjoint",
    )(near_count, near, mid, *columns, u_factor, v_factor, blocks)
    pair = jax.ShapeDtypeStruct((2, 8192), BF16)
    terms = pl.pallas_call(
        chip_sum_kernel,
        in_specs=[VMEM] * 2,
        out_specs=[VMEM] * 4,
        out_shape=[jax.ShapeDtypeStruct(pair.shape, F32)] + [pair] * 3,
        compiler_params=params(4),
        name="chip_sum",
    )(kept, over_sta(swapped, 1))
    gradient = terms[0]
    for t in range(1, 4):
        gradient = gradient + over_sta(terms[t], 2 * t).astype(F32)
    return (predicted, gradient)


def solution(mesh):
    return jax.shard_map(
        body,
        mesh=mesh,
        in_specs=(
            P("sta", "cel"),
            P(None, "sta"),
            P(None, "cel"),
            P("sta"),
            P("sta", "cel", None, None),
            P("sta", None),
            P("sta", "cel", None, None),
            P("sta", "cel", None, None, None),
            P("sta", "cel", None, None, None),
        ),
        out_specs=(P(None, ("sta", "cel")), P("sta", "cel")),
        check_vma=False,
    )
```

```python
import functools

import jax
import jax.numpy as jnp
from jax import lax
from jax.experimental import pallas as pl
from jax.experimental.pallas import tpu as pltpu
from jax.sharding import PartitionSpec as P

VOLUME = 0.03125
FIELD = (0.17101, 0.46985, -0.86603)
ROOT = (3.0 * VOLUME) ** 0.5

TILE = 256
VECS = 16
GROUP = 8
MIB = 1 << 20
WIDE = 8
TALL = 4
F32 = jnp.float32
BF16 = jnp.bfloat16

SMEM = pl.BlockSpec(memory_space=pltpu.SMEM)
VMEM = pl.BlockSpec(memory_space=pltpu.VMEM)
ANY = pl.BlockSpec(memory_space=pl.ANY)


def split3(x):
    high = x.astype(BF16).astype(F32)
    rest = x - high
    middle = rest.astype(BF16).astype(F32)
    return high, middle, rest - middle


def near_kernel(counts, pairs, stations, cells, out, station_rows, cell_rows):
    def station_chunk(i, carry):
        at = pl.ds(pl.multiple_of(i * 2048, 2048), 2048)
        x, y, z = (stations[d : d + 1, at] for d in range(3))
        station_rows[0:1, at] = x
        station_rows[1:2, at] = y
        station_rows[2:3, at] = z
        station_rows[3:4, at] = x * x + y * y + z * z
        station_rows[4:5, at] = ROOT * (FIELD[0] * x + FIELD[1] * y + FIELD[2] * z)
        station_rows[5:6, at] = jnp.ones_like(x)
        station_rows[6:8, at] = jnp.zeros((2, 2048), F32)
        return carry

    lax.fori_loop(0, stations.shape[1] // 2048, station_chunk, 0)

    def cell_chunk(i, carry):
        at = pl.ds(pl.multiple_of(i * TILE, TILE), TILE)
        x, y, z = (cells[d : d + 1, at] for d in range(3))
        zero = jnp.zeros_like(x)
        one = jnp.ones_like(x)
        square = x * x + y * y + z * z
        along = -ROOT * (FIELD[0] * x + FIELD[1] * y + FIELD[2] * z)
        lines = lax.broadcasted_iota(jnp.int32, (8, TILE), 0)

        def stack(values):
            total = jnp.zeros((8, TILE), F32)
            for line, value in values:
                total = jnp.where(lines == line, value, total)
            return total

        wide = stack(((0, -2.0 * x), (1, -2.0 * y), (2, -2.0 * z), (3, one), (5, square)))
        flat = stack(((4, one), (5, along)))
        for position, block in enumerate((wide, flat)):
            h, m, l = split3(block)
            turned = jnp.concatenate((h, h, h, m, m, l), axis=0).T
            cell_rows[i, position * TILE : (position + 1) * TILE, :] = turned.astype(BF16)
        return carry

    lax.fori_loop(0, cells.shape[1] // TILE, cell_chunk, 0)

    def step_blocks(step, carry):
        for j in range(GROUP):
            row = pairs[0, step * GROUP + j]
            column = pairs[1, step * GROUP + j]
            at = pl.ds(pl.multiple_of(row * TILE, TILE), TILE)
            h, m, l = split3(station_rows[:, at])
            right = jnp.concatenate((h, m, l, h, m, h), axis=0).astype(BF16)
            both = jnp.dot(cell_rows[column], right, preferred_element_type=F32)
            distance, along = both[:TILE], both[TILE:]
            inverse = lax.rsqrt(distance)
            square = inverse * inverse
            out[step * GROUP + j] = ((along * along * square - VOLUME) * (square * inverse)).astype(BF16)
        return carry

    lax.fori_loop(0, near_groups(counts), step_blocks, 0)


def block_mask():
    lines = lax.broadcasted_iota(jnp.int32, (GROUP * VECS, TILE), 0) // VECS
    lanes = lax.broadcasted_iota(jnp.int32, (GROUP * VECS, TILE), 1) // (TILE // GROUP)
    return lines == lanes


def near_groups(counts):
    return counts[0, lax.axis_index("cel")] // GROUP


def contract(a, b, dim):
    return lax.dot_general(a, b, (((1,), (dim,)), ((), ())), preferred_element_type=F32)


def lanes_of(column):
    return pl.ds(pl.multiple_of(column * TILE, TILE), TILE)


def place(row):
    share = row >> 2
    return (share & (WIDE - 1)) * TALL + (share >> 3), lanes_of(row & 3)


def forward_kernel(counts, near, mid, *refs):
    parts = refs[:4]
    u_ref, v_ref, blocks = refs[4:7]
    out, stacked, vectors, total = refs[7:]
    for k in range(4):
        stacked[4 * k : 4 * k + 4, :] = parts[k][...].astype(F32)
    vectors[...] = stacked[...].astype(BF16)
    total[...] = jnp.zeros_like(total)
    mask = block_mask()

    def mid_step(i, carry):
        sums = []
        for q in range(4):
            g = i * 4 + q
            source = jnp.concatenate(
                [vectors[:, lanes_of(mid[1, g * GROUP + j])] for j in range(GROUP)], axis=0
            )
            reduced = contract(source, v_ref[g], 1)
            reduced = jnp.where(mask, reduced, 0.0).astype(BF16)
            sums.append(contract(reduced, u_ref[g], 0))
        for q in range(4):
            for j in range(GROUP):
                slot, lanes = place(mid[0, (i * 4 + q) * GROUP + j])
                total[slot, :, lanes] += sums[q][j * VECS : (j + 1) * VECS]
        return carry

    lax.fori_loop(0, u_ref.shape[0] // 4, mid_step, 0)

    def near_step(g, carry):
        sums = [
            contract(vectors[:, lanes_of(near[1, g * GROUP + j])], blocks[g * GROUP + j], 0)
            for j in range(GROUP)
        ]
        for j in range(GROUP):
            slot, lanes = place(near[0, g * GROUP + j])
            total[slot, :, lanes] += sums[j]
        return carry

    lax.fori_loop(0, near_groups(counts), near_step, 0)
    out[...] = total[...].astype(BF16)


def sum_of(parts):
    total = parts[0].astype(F32)
    for k in range(1, parts.shape[0]):
        total = total + parts[k].astype(F32)
    return total


def share_sum_kernel(parts, out):
    out[...] = sum_of(parts).astype(BF16)


def weigh_kernel(parts, weights, predicted, weighted):
    sta, cel = lax.axis_index("sta"), lax.axis_index("cel")
    total = sum_of(parts)
    share = weights[pl.ds(pl.multiple_of(cel * 8, 8), 8), :]
    for r in range(8):
        at = slice(r * 128, (r + 1) * 128)
        value = (total[:, at] * share[r : r + 1, :]).astype(BF16)
        for k in range(TALL):
            weighted[k, :, at] = value
    for place_of in range(8):

        @pl.when(sta == place_of)
        def _():
            for k in range(8):
                line = 2 * (k ^ place_of)
                predicted[line : line + 2, :] = total[2 * k : 2 * k + 2]


def copies_kernel(column, out):
    for i in range(WIDE):
        out[i] = column[...]


def adjoint_kernel(counts, near, mid, data, u_ref, v_ref, blocks, kept, swapped, total):
    total[...] = jnp.zeros_like(total)
    mask = block_mask()

    def station_tile(row):
        slot, lanes = place(row)
        return data[slot, :, lanes]

    def mid_step(i, carry):
        sums = []
        for q in range(4):
            g = i * 4 + q
            source = jnp.concatenate(
                [station_tile(mid[0, g * GROUP + j]) for j in range(GROUP)], axis=0
            )
            pulled = contract(source, u_ref[g], 1)
            pulled = jnp.where(mask, pulled, 0.0).astype(BF16)
            sums.append(contract(pulled, v_ref[g], 0))
        for q in range(4):
            for j in range(GROUP):
                lanes = lanes_of(mid[1, (i * 4 + q) * GROUP + j])
                total[:, lanes] += sums[q][j * VECS : (j + 1) * VECS]
        return carry

    lax.fori_loop(0, u_ref.shape[0] // 4, mid_step, 0)

    def near_step(g, carry):
        sums = [
            contract(station_tile(near[0, g * GROUP + j]), blocks[g * GROUP + j], 1)
            for j in range(GROUP)
        ]
        for j in range(GROUP):
            total[:, lanes_of(near[1, g * GROUP + j])] += sums[j]
        return carry

    lax.fori_loop(0, near_groups(counts), near_step, 0)
    for t in range(4):
        kept[2 * t : 2 * t + 2, :] = total[4 * t : 4 * t + 2, :]
    swapped[...] = jnp.concatenate(
        [total[4 * t + 2 : 4 * t + 4, :] for t in range(4)], axis=0
    ).astype(BF16)


def chip_sum_kernel(kept, swapped, out):
    total = kept[...] + swapped[...].astype(F32)
    chip = lax.axis_index("sta") // 2
    for place_of in range(4):

        @pl.when(chip == place_of)
        def _():
            for t in range(4):
                out[t ^ place_of] = total[2 * t : 2 * t + 2].astype(BF16)


def params(mib):
    return pltpu.CompilerParams(vmem_limit_bytes=mib * MIB)


def body(
    model_vectors, station_xyz, cell_xyz, weights, near_pairs, near_count, mid_pairs, mid_u, mid_v
):
    slots = near_pairs.shape[2]
    near = near_pairs[0, 0].T
    mid = mid_pairs[0, 0].T
    u_factor = mid_u.reshape(-1, TILE, TILE)
    v_factor = mid_v.reshape(-1, TILE, TILE)

    def over_sta(x, k):
        return lax.ppermute(x, "sta", [(i, i ^ k) for i in range(8)])

    wide_groups = [[WIDE * h + w for w in range(WIDE)] for h in range(TALL)]
    tall_groups = [[WIDE * h + w for h in range(TALL)] for w in range(WIDE)]
    chip_groups = [[2 * x + core for x in range(4)] for core in range(2)]

    def trade(x, axis, groups):
        return lax.all_to_all(x, axis, 0, 0, axis_index_groups=groups)

    chip_vectors = jnp.concatenate((model_vectors, over_sta(model_vectors, 1)), axis=0)
    vector_parts = [chip_vectors] + [over_sta(chip_vectors, 2 * k) for k in range(1, 4)]

    blocks = pl.pallas_call(
        near_kernel,
        in_specs=[SMEM] * 2 + [VMEM] * 2,
        out_specs=VMEM,
        out_shape=jax.ShapeDtypeStruct((slots, TILE, TILE), BF16),
        scratch_shapes=[
            pltpu.VMEM((8, station_xyz.shape[1]), F32),
            pltpu.VMEM((cell_xyz.shape[1] // TILE, 2 * TILE, 48), BF16),
        ],
        compiler_params=params(24),
        cost_estimate=pl.CostEstimate(
            flops=slots * 2 * 512 * 48 * 256, bytes_accessed=10 * MIB, transcendentals=slots * 65536
        ),
        name="near_blocks",
    )(near_count, near, station_xyz, cell_xyz)

    wide = jax.ShapeDtypeStruct((WIDE, TALL, VECS, 1024), BF16)
    tall = jax.ShapeDtypeStruct((TALL, VECS, 1024), BF16)
    shares = pl.pallas_call(
        forward_kernel,
        in_specs=[SMEM] * 3 + [VMEM] * 7,
        out_specs=VMEM,
        out_shape=jax.ShapeDtypeStruct((32, VECS, 1024), BF16),
        scratch_shapes=[
            pltpu.VMEM((VECS, 8192), F32),
            pltpu.VMEM((VECS, 8192), BF16),
            pltpu.VMEM((32, VECS, 1024), F32),
        ],
        compiler_params=params(24),
        name="forward",
    )(near_count, near, mid, *vector_parts, u_factor, v_factor, blocks)

    sums = pl.pallas_call(
        share_sum_kernel,
        in_specs=[VMEM],
        out_specs=VMEM,
        out_shape=tall,
        compiler_params=params(8),
        name="share_sum",
    )(trade(shares.reshape(wide.shape), "cel", wide_groups))
    predicted, weighted = pl.pallas_call(
        weigh_kernel,
        in_specs=[VMEM] * 2,
        out_specs=[VMEM] * 2,
        out_shape=[jax.ShapeDtypeStruct((VECS, 1024), F32), tall],
        compiler_params=params(4),
        name="weigh",
    )(trade(sums, "cel", tall_groups), weights.reshape(-1, 128))

    copies = pl.pallas_call(
        copies_kernel,
        in_specs=[VMEM],
        out_specs=VMEM,
        out_shape=wide,
        compiler_params=params(8),
        name="copies",
    )(trade(weighted, "cel", tall_groups))
    data = trade(copies, "cel", wide_groups).reshape(32, VECS, 1024)

    lines = jax.ShapeDtypeStruct((8, 8192), BF16)
    kept, swapped = pl.pallas_call(
        adjoint_kernel,
        in_specs=[SMEM] * 3 + [VMEM] * 4,
        out_specs=[VMEM] * 2,
        out_shape=[jax.ShapeDtypeStruct(lines.shape, F32), lines],
        scratch_shapes=[pltpu.VMEM((VECS, 8192), F32)],
        compiler_params=params(24),
        name="adjoint",
    )(near_count, near, mid, data, u_factor, v_factor, blocks)
    terms = pl.pallas_call(
        chip_sum_kernel,
        in_specs=[VMEM] * 2,
        out_specs=VMEM,
        out_shape=jax.ShapeDtypeStruct((4, 2, 8192), BF16),
        compiler_params=params(4),
        name="chip_sum",
    )(kept, over_sta(swapped, 1))
    gradient = jnp.sum(trade(terms, "sta", chip_groups).astype(F32), axis=0)
    return (predicted, gradient)


def solution(mesh):
    return jax.shard_map(
        body,
        mesh=mesh,
        in_specs=(
            P("sta", "cel"),
            P(None, "sta"),
            P(None, "cel"),
            P("sta"),
            P("sta", "cel", None, None),
            P("sta", None),
            P("sta", "cel", None, None),
            P("sta", "cel", None, None, None),
            P("sta", "cel", None, None, None),
        ),
        out_specs=(P(None, ("sta", "cel")), P("sta", "cel")),
        check_vma=False,
    )
```

```python
import functools

import jax
import jax.numpy as jnp
from jax import lax
from jax.experimental import pallas as pl
from jax.experimental.pallas import tpu as pltpu
from jax.sharding import PartitionSpec as P

VOLUME = 0.03125
FIELD = (0.17101, 0.46985, -0.86603)
ROOT = (3.0 * VOLUME) ** 0.5

TILE = 256
VECS = 16
GROUP = 8
MIB = 1 << 20
WIDE = 8
TALL = 4
HALF = 4
F32 = jnp.float32
BF16 = jnp.bfloat16

SMEM = pl.BlockSpec(memory_space=pltpu.SMEM)
VMEM = pl.BlockSpec(memory_space=pltpu.VMEM)
HBM = pl.BlockSpec(memory_space=pltpu.HBM)


def split3(x):
    high = x.astype(BF16).astype(F32)
    rest = x - high
    middle = rest.astype(BF16).astype(F32)
    return high, middle, rest - middle


def stack(lines, values):
    total = jnp.zeros(lines.shape, F32)
    for line, value in values:
        total = jnp.where(lines == line, value, total)
    return total


def field_of(x, y, z):
    return ROOT * (FIELD[0] * x + FIELD[1] * y + FIELD[2] * z)


def near_group(g, pairs, stations, features, out, first):
    lines = lax.broadcasted_iota(jnp.int32, (8, TILE), 0)
    for j in range(GROUP):
        at = lanes_of(pairs[0, g * GROUP + j])
        x, y, z = (stations[d : d + 1, at] for d in range(3))
        one = jnp.ones_like(x)
        wide = stack(lines, ((0, x), (1, y), (2, z), (3, x * x + y * y + z * z), (5, one)))
        flat = stack(lines, ((3, field_of(x, y, z)), (6, one)))
        left = features[pairs[1, g * GROUP + j]]

        def product(block):
            h, m, l = split3(block)
            right = jnp.concatenate((h, m, l, h, m, h), axis=0).astype(BF16)
            return jnp.dot(left, right, preferred_element_type=F32)

        inverse = lax.rsqrt(product(wide))
        along = product(flat)
        square = inverse * inverse
        out[(g - first) * GROUP + j] = (
            (along * along * square - VOLUME) * (square * inverse)
        ).astype(BF16)


def near_first_kernel(counts, pairs, station_hbm, cell_hbm, out, features, stations, cells, sem):
    fetches = [
        pltpu.make_async_copy(cell_hbm, cells, sem.at[0]),
        pltpu.make_async_copy(station_hbm, stations, sem.at[1]),
    ]
    for fetch in fetches:
        fetch.start()
    fetches[0].wait()

    def cell_chunk(i, carry):
        lines = lax.broadcasted_iota(jnp.int32, (8, TILE), 0)
        for q in range(4):
            at = lanes_of(i * 4 + q)
            x, y, z = (cells[d : d + 1, at] for d in range(3))
            square = x * x + y * y + z * z
            block = stack(
                lines,
                (
                    (0, -2.0 * x),
                    (1, -2.0 * y),
                    (2, -2.0 * z),
                    (3, jnp.ones_like(x)),
                    (5, square),
                    (6, -field_of(x, y, z)),
                ),
            )
            h, m, l = split3(block)
            features[i * 4 + q] = jnp.concatenate((h, h, h, m, m, l), axis=0).T.astype(BF16)
        return carry

    lax.fori_loop(0, features.shape[0] // 4, cell_chunk, 0)
    fetches[1].wait()

    def step(g, carry):
        near_group(g, pairs, stations, features, out, 0)
        return carry

    lax.fori_loop(0, jnp.minimum(near_groups(counts), HALF), step, 0)


def near_second_kernel(counts, pairs, stations, features, out):
    def step(g, carry):
        near_group(g, pairs, stations, features, out, HALF)
        return carry

    lax.fori_loop(HALF, near_groups(counts), step, 0)


def block_mask():
    lines = lax.broadcasted_iota(jnp.int32, (GROUP * VECS, TILE), 0) // VECS
    lanes = lax.broadcasted_iota(jnp.int32, (GROUP * VECS, TILE), 1) // (TILE // GROUP)
    return lines == lanes


def near_groups(counts):
    return counts[0, lax.axis_index("cel")] // GROUP


def contract(a, b, dim):
    return lax.dot_general(a, b, (((1,), (dim,)), ((), ())), preferred_element_type=F32)


def lanes_of(column):
    return pl.ds(pl.multiple_of(column * TILE, TILE), TILE)


def place(row):
    share = row >> 2
    return (share & (WIDE - 1)) * TALL + (share >> 3), lanes_of(row & 3)


def forward_kernel(counts, near, mid, *refs):
    parts = refs[:4]
    u_ref, v_ref, first_blocks, second_blocks, out, stacked, vectors, total = refs[4:]
    for k in range(4):
        stacked[4 * k : 4 * k + 4, :] = parts[k][...].astype(F32)
    vectors[...] = stacked[...].astype(BF16)
    total[...] = jnp.zeros_like(total)
    mask = block_mask()

    sums = []
    for g in range(u_ref.shape[0]):
        source = jnp.concatenate(
            [vectors[:, lanes_of(mid[1, g * GROUP + j])] for j in range(GROUP)], axis=0
        )
        reduced = contract(source, v_ref[g], 1)
        reduced = jnp.where(mask, reduced, 0.0).astype(BF16)
        sums.append(contract(reduced, u_ref[g], 0))
    for g in range(u_ref.shape[0]):
        for j in range(GROUP):
            slot, lanes = place(mid[0, g * GROUP + j])
            total[slot, :, lanes] += sums[g][j * VECS : (j + 1) * VECS]

    def near_step(g, carry, blocks, first):
        sums = [
            contract(vectors[:, lanes_of(near[1, g * GROUP + j])], blocks[(g - first) * GROUP + j], 0)
            for j in range(GROUP)
        ]
        for j in range(GROUP):
            slot, lanes = place(near[0, g * GROUP + j])
            total[slot, :, lanes] += sums[j]
        return carry

    groups = near_groups(counts)
    first_step = functools.partial(near_step, blocks=first_blocks, first=0)
    second_step = functools.partial(near_step, blocks=second_blocks, first=HALF)
    lax.fori_loop(0, jnp.minimum(groups, HALF), first_step, 0)
    lax.fori_loop(HALF, groups, second_step, 0)
    out[...] = total[...].astype(BF16)


def sum_of(parts):
    total = parts[0].astype(F32)
    for k in range(1, parts.shape[0]):
        total = total + parts[k].astype(F32)
    return total


def share_sum_kernel(parts, out):
    out[...] = sum_of(parts).astype(BF16)


def weigh_kernel(parts, weights, predicted, weighted):
    sta, cel = lax.axis_index("sta"), lax.axis_index("cel")
    total = sum_of(parts)
    share = weights[pl.ds(pl.multiple_of(cel * 8, 8), 8), :]
    for r in range(8):
        at = slice(r * 128, (r + 1) * 128)
        value = (total[:, at] * share[r : r + 1, :]).astype(BF16)
        for k in range(TALL):
            weighted[k, :, at] = value
    for place_of in range(8):

        @pl.when(sta == place_of)
        def _():
            for k in range(8):
                line = 2 * (k ^ place_of)
                predicted[line : line + 2, :] = total[2 * k : 2 * k + 2]


def copies_kernel(column, out):
    for i in range(WIDE):
        out[i] = column[...]


def adjoint_kernel(
    counts, near, mid, data, u_ref, v_ref, first_blocks, second_blocks, kept, swapped, total
):
    total[...] = jnp.zeros_like(total)
    mask = block_mask()

    def station_tile(row):
        slot, lanes = place(row)
        return data[slot, :, lanes]

    sums = []
    for g in range(u_ref.shape[0]):
        source = jnp.concatenate(
            [station_tile(mid[0, g * GROUP + j]) for j in range(GROUP)], axis=0
        )
        pulled = contract(source, u_ref[g], 1)
        pulled = jnp.where(mask, pulled, 0.0).astype(BF16)
        sums.append(contract(pulled, v_ref[g], 0))
    for g in range(u_ref.shape[0]):
        for j in range(GROUP):
            lanes = lanes_of(mid[1, g * GROUP + j])
            total[:, lanes] += sums[g][j * VECS : (j + 1) * VECS]

    def near_step(g, carry, blocks, first):
        sums = [
            contract(station_tile(near[0, g * GROUP + j]), blocks[(g - first) * GROUP + j], 1)
            for j in range(GROUP)
        ]
        for j in range(GROUP):
            total[:, lanes_of(near[1, g * GROUP + j])] += sums[j]
        return carry

    groups = near_groups(counts)
    first_step = functools.partial(near_step, blocks=first_blocks, first=0)
    second_step = functools.partial(near_step, blocks=second_blocks, first=HALF)
    lax.fori_loop(0, jnp.minimum(groups, HALF), first_step, 0)
    lax.fori_loop(HALF, groups, second_step, 0)
    for t in range(4):
        kept[2 * t : 2 * t + 2, :] = total[4 * t : 4 * t + 2, :]
    swapped[...] = jnp.concatenate(
        [total[4 * t + 2 : 4 * t + 4, :] for t in range(4)], axis=0
    ).astype(BF16)


def chip_sum_kernel(kept, swapped, *outs):
    total = kept[...] + swapped[...].astype(F32)
    for t in range(4):
        outs[t][...] = total[2 * t : 2 * t + 2].astype(outs[t].dtype)


def params(mib):
    return pltpu.CompilerParams(vmem_limit_bytes=mib * MIB)


def body(
    model_vectors, station_xyz, cell_xyz, weights, near_pairs, near_count, mid_pairs, mid_u, mid_v
):
    slots = near_pairs.shape[2]
    near = near_pairs[0, 0].T
    mid = mid_pairs[0, 0].T
    u_factor = mid_u.reshape(-1, TILE, TILE)
    v_factor = mid_v.reshape(-1, TILE, TILE)

    def over_sta(x, k):
        return lax.ppermute(x, "sta", [(i, i ^ k) for i in range(8)])

    wide_groups = [[WIDE * h + w for w in range(WIDE)] for h in range(TALL)]
    tall_groups = [[WIDE * h + w for h in range(TALL)] for w in range(WIDE)]

    def trade(x, axis, groups):
        return lax.all_to_all(x, axis, 0, 0, axis_index_groups=groups)

    half = HALF * GROUP
    cell_tiles = cell_xyz.shape[1] // TILE
    other_vectors = over_sta(model_vectors, 1)
    first_blocks, features, stations = pl.pallas_call(
        near_first_kernel,
        in_specs=[SMEM] * 2 + [HBM] * 2,
        out_specs=[VMEM] * 3,
        out_shape=[
            jax.ShapeDtypeStruct((half, TILE, TILE), BF16),
            jax.ShapeDtypeStruct((cell_tiles, TILE, 48), BF16),
            jax.ShapeDtypeStruct(station_xyz.shape, F32),
        ],
        scratch_shapes=[pltpu.VMEM(cell_xyz.shape, F32), pltpu.SemaphoreType.DMA((2,))],
        compiler_params=params(16),
        cost_estimate=pl.CostEstimate(
            flops=half * 2 * 512 * 48 * 256, bytes_accessed=6 * MIB, transcendentals=half * 65536
        ),
        name="near_first",
    )(near_count, near, station_xyz, cell_xyz)
    other_vectors, features = lax.optimization_barrier((other_vectors, features))
    chip_vectors = jnp.concatenate((model_vectors, other_vectors), axis=0)
    vector_parts = [chip_vectors] + [over_sta(chip_vectors, 2 * k) for k in range(1, 4)]
    second_blocks = pl.pallas_call(
        near_second_kernel,
        in_specs=[SMEM] * 2 + [VMEM] * 2,
        out_specs=VMEM,
        out_shape=jax.ShapeDtypeStruct((slots - half, TILE, TILE), BF16),
        compiler_params=params(16),
        cost_estimate=pl.CostEstimate(
            flops=half * 2 * 512 * 48 * 256, bytes_accessed=6 * MIB, transcendentals=half * 65536
        ),
        name="near_second",
    )(near_count, near, stations, features)

    wide = jax.ShapeDtypeStruct((WIDE, TALL, VECS, 1024), BF16)
    tall = jax.ShapeDtypeStruct((TALL, VECS, 1024), BF16)
    shares = pl.pallas_call(
        forward_kernel,
        in_specs=[SMEM] * 3 + [VMEM] * 8,
        out_specs=VMEM,
        out_shape=jax.ShapeDtypeStruct((32, VECS, 1024), BF16),
        scratch_shapes=[
            pltpu.VMEM((VECS, 8192), F32),
            pltpu.VMEM((VECS, 8192), BF16),
            pltpu.VMEM((32, VECS, 1024), F32),
        ],
        compiler_params=params(24),
        name="forward",
    )(near_count, near, mid, *vector_parts, u_factor, v_factor, first_blocks, second_blocks)

    sums = pl.pallas_call(
        share_sum_kernel,
        in_specs=[VMEM],
        out_specs=VMEM,
        out_shape=tall,
        compiler_params=params(8),
        name="share_sum",
    )(trade(shares.reshape(wide.shape), "cel", wide_groups))
    predicted, weighted = pl.pallas_call(
        weigh_kernel,
        in_specs=[VMEM] * 2,
        out_specs=[VMEM] * 2,
        out_shape=[jax.ShapeDtypeStruct((VECS, 1024), F32), tall],
        compiler_params=params(4),
        name="weigh",
    )(trade(sums, "cel", tall_groups), weights.reshape(-1, 128))

    copies = pl.pallas_call(
        copies_kernel,
        in_specs=[VMEM],
        out_specs=VMEM,
        out_shape=wide,
        compiler_params=params(8),
        name="copies",
    )(trade(weighted, "cel", tall_groups))
    data = trade(copies, "cel", wide_groups).reshape(32, VECS, 1024)

    lines = jax.ShapeDtypeStruct((8, 8192), BF16)
    kept, swapped = pl.pallas_call(
        adjoint_kernel,
        in_specs=[SMEM] * 3 + [VMEM] * 5,
        out_specs=[VMEM] * 2,
        out_shape=[jax.ShapeDtypeStruct(lines.shape, F32), lines],
        scratch_shapes=[pltpu.VMEM((VECS, 8192), F32)],
        compiler_params=params(24),
        name="adjoint",
    )(near_count, near, mid, data, u_factor, v_factor, first_blocks, second_blocks)
    pair = jax.ShapeDtypeStruct((2, 8192), BF16)
    terms = pl.pallas_call(
        chip_sum_kernel,
        in_specs=[VMEM] * 2,
        out_specs=[VMEM] * 4,
        out_shape=[jax.ShapeDtypeStruct(pair.shape, F32)] + [pair] * 3,
        compiler_params=params(4),
        name="chip_sum",
    )(kept, over_sta(swapped, 1))
    gradient = terms[0]
    for t in range(1, 4):
        gradient = gradient + over_sta(terms[t], 2 * t).astype(F32)
    return (predicted, gradient)


def solution(mesh):
    return jax.shard_map(
        body,
        mesh=mesh,
        in_specs=(
            P("sta", "cel"),
            P(None, "sta"),
            P(None, "cel"),
            P("sta"),
            P("sta", "cel", None, None),
            P("sta", None),
            P("sta", "cel", None, None),
            P("sta", "cel", None, None, None),
            P("sta", "cel", None, None, None),
        ),
        out_specs=(P(None, ("sta", "cel")), P("sta", "cel")),
        check_vma=False,
    )
```

```python
import functools

import jax
import jax.numpy as jnp
from jax import lax
from jax.experimental import pallas as pl
from jax.experimental.pallas import tpu as pltpu
from jax.sharding import PartitionSpec as P

VOLUME = 0.03125
FIELD = (0.17101, 0.46985, -0.86603)
ROOT = (3.0 * VOLUME) ** 0.5

TILE = 256
VECS = 16
GROUP = 8
MIB = 1 << 20
WIDE = 8
TALL = 4
HALF = 4
F32 = jnp.float32
BF16 = jnp.bfloat16

SMEM = pl.BlockSpec(memory_space=pltpu.SMEM)
VMEM = pl.BlockSpec(memory_space=pltpu.VMEM)
HBM = pl.BlockSpec(memory_space=pltpu.HBM)


def split3(x):
    high = x.astype(BF16).astype(F32)
    rest = x - high
    middle = rest.astype(BF16).astype(F32)
    return high, middle, rest - middle


def stack(lines, values):
    total = jnp.zeros(lines.shape, F32)
    for line, value in values:
        total = jnp.where(lines == line, value, total)
    return total


def field_of(x, y, z):
    return ROOT * (FIELD[0] * x + FIELD[1] * y + FIELD[2] * z)


def near_group(g, pairs, stations, features, out, first):
    lines = lax.broadcasted_iota(jnp.int32, (8, TILE), 0)
    for j in range(GROUP):
        at = lanes_of(pairs[0, g * GROUP + j])
        x, y, z = (stations[d : d + 1, at] for d in range(3))
        one = jnp.ones_like(x)
        wide = stack(lines, ((0, x), (1, y), (2, z), (3, x * x + y * y + z * z), (5, one)))
        flat = stack(lines, ((3, field_of(x, y, z)), (6, one)))
        left = features[pairs[1, g * GROUP + j]]

        def product(block):
            h, m, l = split3(block)
            right = jnp.concatenate((h, m, l, h, m, h), axis=0).astype(BF16)
            return jnp.dot(left, right, preferred_element_type=F32)

        inverse = lax.rsqrt(product(wide))
        along = product(flat)
        square = inverse * inverse
        out[(g - first) * GROUP + j] = (
            (along * along * square - VOLUME) * (square * inverse)
        ).astype(BF16)


def near_first_kernel(counts, pairs, station_hbm, cell_hbm, out, features, stations, cells, sem):
    fetches = [
        pltpu.make_async_copy(cell_hbm, cells, sem.at[0]),
        pltpu.make_async_copy(station_hbm, stations, sem.at[1]),
    ]
    for fetch in fetches:
        fetch.start()
    fetches[0].wait()

    def cell_chunk(i, carry):
        lines = lax.broadcasted_iota(jnp.int32, (8, TILE), 0)
        for q in range(4):
            at = lanes_of(i * 4 + q)
            x, y, z = (cells[d : d + 1, at] for d in range(3))
            square = x * x + y * y + z * z
            block = stack(
                lines,
                (
                    (0, -2.0 * x),
                    (1, -2.0 * y),
                    (2, -2.0 * z),
                    (3, jnp.ones_like(x)),
                    (5, square),
                    (6, -field_of(x, y, z)),
                ),
            )
            h, m, l = split3(block)
            features[i * 4 + q] = jnp.concatenate((h, h, h, m, m, l), axis=0).T.astype(BF16)
        return carry

    lax.fori_loop(0, features.shape[0] // 4, cell_chunk, 0)
    fetches[1].wait()

    def step(g, carry):
        near_group(g, pairs, stations, features, out, 0)
        return carry

    lax.fori_loop(0, jnp.minimum(near_groups(counts), HALF), step, 0)


def near_second_kernel(counts, pairs, stations, features, out):
    def step(g, carry):
        near_group(g, pairs, stations, features, out, HALF)
        return carry

    lax.fori_loop(HALF, near_groups(counts), step, 0)


def block_mask():
    lines = lax.broadcasted_iota(jnp.int32, (GROUP * VECS, TILE), 0) // VECS
    lanes = lax.broadcasted_iota(jnp.int32, (GROUP * VECS, TILE), 1) // (TILE // GROUP)
    return lines == lanes


def near_groups(counts):
    return counts[0, lax.axis_index("cel")] // GROUP


def contract(a, b, dim):
    return lax.dot_general(a, b, (((1,), (dim,)), ((), ())), preferred_element_type=F32)


def lanes_of(column):
    return pl.ds(pl.multiple_of(column * TILE, TILE), TILE)


def place(row):
    share = row >> 2
    return (share & (WIDE - 1)) * TALL + (share >> 3), lanes_of(row & 3)


def forward_kernel(counts, near, mid, *refs):
    parts = refs[:4]
    u_ref, v_ref, first_blocks, second_blocks, out, stacked, vectors, total = refs[4:]
    for k in range(4):
        stacked[4 * k : 4 * k + 4, :] = parts[k][...].astype(F32)
    vectors[...] = stacked[...].astype(BF16)
    total[...] = jnp.zeros_like(total)
    mask = block_mask()

    sums = []
    for g in range(u_ref.shape[0]):
        source = jnp.concatenate(
            [vectors[:, lanes_of(mid[1, g * GROUP + j])] for j in range(GROUP)], axis=0
        )
        reduced = contract(source, v_ref[g], 1)
        reduced = jnp.where(mask, reduced, 0.0).astype(BF16)
        sums.append(contract(reduced, u_ref[g], 0))
    for g in range(u_ref.shape[0]):
        for j in range(GROUP):
            slot, lanes = place(mid[0, g * GROUP + j])
            total[slot, :, lanes] += sums[g][j * VECS : (j + 1) * VECS]

    def near_step(g, carry, blocks, first):
        sums = [
            contract(vectors[:, lanes_of(near[1, g * GROUP + j])], blocks[(g - first) * GROUP + j], 0)
            for j in range(GROUP)
        ]
        for j in range(GROUP):
            slot, lanes = place(near[0, g * GROUP + j])
            total[slot, :, lanes] += sums[j]
        return carry

    groups = near_groups(counts)
    first_step = functools.partial(near_step, blocks=first_blocks, first=0)
    second_step = functools.partial(near_step, blocks=second_blocks, first=HALF)
    lax.fori_loop(0, jnp.minimum(groups, HALF), first_step, 0)
    lax.fori_loop(HALF, groups, second_step, 0)
    out[...] = total[...].astype(BF16)


def sum_of(parts):
    total = parts[0].astype(F32)
    for k in range(1, parts.shape[0]):
        total = total + parts[k].astype(F32)
    return total


def share_sum_kernel(parts, out):
    total = sum_of(parts).astype(BF16)
    for k in range(TALL):
        out[k] = total


def weigh_kernel(parts, weights, predicted, weighted):
    sta, cel = lax.axis_index("sta"), lax.axis_index("cel")
    for h in range(TALL):
        total = parts[0, h].astype(F32)
        for k in range(1, TALL):
            total = total + parts[k, h].astype(F32)

        @pl.when(cel // WIDE == h)
        def _():
            for place_of in range(8):

                @pl.when(sta == place_of)
                def _():
                    for k in range(8):
                        line = 2 * (k ^ place_of)
                        predicted[line : line + 2, :] = total[2 * k : 2 * k + 2]

        share = h * WIDE + cel % WIDE
        scale = weights[pl.ds(pl.multiple_of(share * 8, 8), 8), :]
        for r in range(8):
            at = slice(r * 128, (r + 1) * 128)
            value = (total[:, at] * scale[r : r + 1, :]).astype(BF16)
            for i in range(WIDE):
                weighted[i, h, :, at] = value


def adjoint_kernel(
    counts, near, mid, data, u_ref, v_ref, first_blocks, second_blocks, kept, swapped, total
):
    total[...] = jnp.zeros_like(total)
    mask = block_mask()

    def station_tile(row):
        slot, lanes = place(row)
        return data[slot, :, lanes]

    sums = []
    for g in range(u_ref.shape[0]):
        source = jnp.concatenate(
            [station_tile(mid[0, g * GROUP + j]) for j in range(GROUP)], axis=0
        )
        pulled = contract(source, u_ref[g], 1)
        pulled = jnp.where(mask, pulled, 0.0).astype(BF16)
        sums.append(contract(pulled, v_ref[g], 0))
    for g in range(u_ref.shape[0]):
        for j in range(GROUP):
            lanes = lanes_of(mid[1, g * GROUP + j])
            total[:, lanes] += sums[g][j * VECS : (j + 1) * VECS]

    def near_step(g, carry, blocks, first):
        sums = [
            contract(station_tile(near[0, g * GROUP + j]), blocks[(g - first) * GROUP + j], 1)
            for j in range(GROUP)
        ]
        for j in range(GROUP):
            total[:, lanes_of(near[1, g * GROUP + j])] += sums[j]
        return carry

    groups = near_groups(counts)
    first_step = functools.partial(near_step, blocks=first_blocks, first=0)
    second_step = functools.partial(near_step, blocks=second_blocks, first=HALF)
    lax.fori_loop(0, jnp.minimum(groups, HALF), first_step, 0)
    lax.fori_loop(HALF, groups, second_step, 0)
    for t in range(4):
        kept[2 * t : 2 * t + 2, :] = total[4 * t : 4 * t + 2, :]
    swapped[...] = jnp.concatenate(
        [total[4 * t + 2 : 4 * t + 4, :] for t in range(4)], axis=0
    ).astype(BF16)


def chip_sum_kernel(kept, swapped, *outs):
    total = kept[...] + swapped[...].astype(F32)
    for t in range(4):
        outs[t][...] = total[2 * t : 2 * t + 2].astype(outs[t].dtype)


def params(mib):
    return pltpu.CompilerParams(vmem_limit_bytes=mib * MIB)


def body(
    model_vectors, station_xyz, cell_xyz, weights, near_pairs, near_count, mid_pairs, mid_u, mid_v
):
    slots = near_pairs.shape[2]
    near = near_pairs[0, 0].T
    mid = mid_pairs[0, 0].T
    u_factor = mid_u.reshape(-1, TILE, TILE)
    v_factor = mid_v.reshape(-1, TILE, TILE)

    def over_sta(x, k):
        return lax.ppermute(x, "sta", [(i, i ^ k) for i in range(8)])

    wide_groups = [[WIDE * h + w for w in range(WIDE)] for h in range(TALL)]
    tall_groups = [[WIDE * h + w for h in range(TALL)] for w in range(WIDE)]

    def trade(x, axis, groups):
        return lax.all_to_all(x, axis, 0, 0, axis_index_groups=groups)

    half = HALF * GROUP
    cell_tiles = cell_xyz.shape[1] // TILE
    other_vectors = over_sta(model_vectors, 1)
    inputs = (near_count, near, station_xyz, cell_xyz)
    first_blocks, features, stations = pl.pallas_call(
        near_first_kernel,
        in_specs=[SMEM] * 2 + [HBM] * 2,
        out_specs=[VMEM] * 3,
        out_shape=[
            jax.ShapeDtypeStruct((half, TILE, TILE), BF16),
            jax.ShapeDtypeStruct((cell_tiles, TILE, 48), BF16),
            jax.ShapeDtypeStruct(station_xyz.shape, F32),
        ],
        scratch_shapes=[pltpu.VMEM(cell_xyz.shape, F32), pltpu.SemaphoreType.DMA((2,))],
        compiler_params=params(16),
        cost_estimate=pl.CostEstimate(
            flops=half * 2 * 512 * 48 * 256, bytes_accessed=6 * MIB, transcendentals=half * 65536
        ),
        name="near_first",
    )(*[pltpu.with_memory_space_constraint(a, pltpu.HBM) for a in inputs])
    other_vectors, features = lax.optimization_barrier((other_vectors, features))
    chip_vectors = jnp.concatenate((model_vectors, other_vectors), axis=0)
    vector_parts = [chip_vectors] + [over_sta(chip_vectors, 2 * k) for k in range(1, 4)]
    second_blocks = pl.pallas_call(
        near_second_kernel,
        in_specs=[SMEM] * 2 + [VMEM] * 2,
        out_specs=VMEM,
        out_shape=jax.ShapeDtypeStruct((slots - half, TILE, TILE), BF16),
        compiler_params=params(16),
        cost_estimate=pl.CostEstimate(
            flops=half * 2 * 512 * 48 * 256, bytes_accessed=6 * MIB, transcendentals=half * 65536
        ),
        name="near_second",
    )(near_count, near, stations, features)

    wide = jax.ShapeDtypeStruct((WIDE, TALL, VECS, 1024), BF16)
    tall = jax.ShapeDtypeStruct((TALL, VECS, 1024), BF16)
    shares = pl.pallas_call(
        forward_kernel,
        in_specs=[SMEM] * 3 + [VMEM] * 8,
        out_specs=VMEM,
        out_shape=jax.ShapeDtypeStruct((32, VECS, 1024), BF16),
        scratch_shapes=[
            pltpu.VMEM((VECS, 8192), F32),
            pltpu.VMEM((VECS, 8192), BF16),
            pltpu.VMEM((32, VECS, 1024), F32),
        ],
        compiler_params=params(24),
        name="forward",
    )(near_count, near, mid, *vector_parts, u_factor, v_factor, first_blocks, second_blocks)

    sums = pl.pallas_call(
        share_sum_kernel,
        in_specs=[VMEM],
        out_specs=VMEM,
        out_shape=jax.ShapeDtypeStruct((TALL, *tall.shape), BF16),
        compiler_params=params(8),
        name="share_sum",
    )(trade(shares.reshape(wide.shape), "cel", wide_groups))
    predicted, weighted = pl.pallas_call(
        weigh_kernel,
        in_specs=[VMEM] * 2,
        out_specs=[VMEM] * 2,
        out_shape=[jax.ShapeDtypeStruct((VECS, 1024), F32), wide],
        compiler_params=params(8),
        name="weigh",
    )(trade(sums, "cel", tall_groups), weights.reshape(-1, 128))
    data = trade(weighted, "cel", wide_groups).reshape(32, VECS, 1024)

    lines = jax.ShapeDtypeStruct((8, 8192), BF16)
    kept, swapped = pl.pallas_call(
        adjoint_kernel,
        in_specs=[SMEM] * 3 + [VMEM] * 5,
        out_specs=[VMEM] * 2,
        out_shape=[jax.ShapeDtypeStruct(lines.shape, F32), lines],
        scratch_shapes=[pltpu.VMEM((VECS, 8192), F32)],
        compiler_params=params(24),
        name="adjoint",
    )(near_count, near, mid, data, u_factor, v_factor, first_blocks, second_blocks)
    pair = jax.ShapeDtypeStruct((2, 8192), BF16)
    terms = pl.pallas_call(
        chip_sum_kernel,
        in_specs=[VMEM] * 2,
        out_specs=[VMEM] * 4,
        out_shape=[jax.ShapeDtypeStruct(pair.shape, F32)] + [pair] * 3,
        compiler_params=params(4),
        name="chip_sum",
    )(kept, over_sta(swapped, 1))
    gradient = terms[0]
    for t in range(1, 4):
        gradient = gradient + over_sta(terms[t], 2 * t).astype(F32)
    return (predicted, gradient)


def solution(mesh):
    return jax.shard_map(
        body,
        mesh=mesh,
        in_specs=(
            P("sta", "cel"),
            P(None, "sta"),
            P(None, "cel"),
            P("sta"),
            P("sta", "cel", None, None),
            P("sta", None),
            P("sta", "cel", None, None),
            P("sta", "cel", None, None, None),
            P("sta", "cel", None, None, None),
        ),
        out_specs=(P(None, ("sta", "cel")), P("sta", "cel")),
        check_vma=False,
    )
```

```python
import functools

import jax
import jax.numpy as jnp
from jax import lax
from jax.experimental import pallas as pl
from jax.experimental.pallas import tpu as pltpu
from jax.sharding import PartitionSpec as P

VOLUME = 0.03125
FIELD = (0.17101, 0.46985, -0.86603)
SHRINK = VOLUME ** (-1.0 / 3.0)
SLOPE = 3.0**0.5

TILE = 256
VECS = 16
GROUP = 8
MIB = 1 << 20
WIDE = 8
TALL = 4
HALF = 4
F32 = jnp.float32
BF16 = jnp.bfloat16

SMEM = pl.BlockSpec(memory_space=pltpu.SMEM)
VMEM = pl.BlockSpec(memory_space=pltpu.VMEM)
HBM = pl.BlockSpec(memory_space=pltpu.HBM)


def split3(x):
    high = x.astype(BF16).astype(F32)
    rest = x - high
    middle = rest.astype(BF16).astype(F32)
    return high, middle, rest - middle


def stack(lines, values):
    total = jnp.zeros(lines.shape, F32)
    for line, value in values:
        total = jnp.where(lines == line, value, total)
    return total


def field_of(x, y, z):
    return SLOPE * (FIELD[0] * x + FIELD[1] * y + FIELD[2] * z)


def near_group(g, pairs, stations, features, out, first):
    lines = lax.broadcasted_iota(jnp.int32, (8, TILE), 0)
    for j in range(GROUP):
        at = lanes_of(pairs[0, g * GROUP + j])
        x, y, z = (SHRINK * stations[d : d + 1, at] for d in range(3))
        one = jnp.ones_like(x)
        wide = stack(lines, ((0, x), (1, y), (2, z), (3, x * x + y * y + z * z), (5, one)))
        flat = stack(lines, ((3, field_of(x, y, z)), (6, one)))
        left = features[pairs[1, g * GROUP + j]]

        def product(block):
            h, m, l = split3(block)
            right = jnp.concatenate((h, m, l, h, m, h), axis=0).astype(BF16)
            return jnp.dot(left, right, preferred_element_type=F32)

        inverse = lax.rsqrt(product(wide))
        along = product(flat)
        square = inverse * inverse
        along = along * square
        out[(g - first) * GROUP + j] = ((along * along - square) * inverse).astype(BF16)


def near_first_kernel(counts, pairs, station_hbm, cell_hbm, out, features, stations, cells, sem):
    fetches = [
        pltpu.make_async_copy(cell_hbm, cells, sem.at[0]),
        pltpu.make_async_copy(station_hbm, stations, sem.at[1]),
    ]
    for fetch in fetches:
        fetch.start()
    fetches[0].wait()

    def cell_chunk(i, carry):
        lines = lax.broadcasted_iota(jnp.int32, (8, TILE), 0)
        for q in range(4):
            at = lanes_of(i * 4 + q)
            x, y, z = (SHRINK * cells[d : d + 1, at] for d in range(3))
            square = x * x + y * y + z * z
            block = stack(
                lines,
                (
                    (0, -2.0 * x),
                    (1, -2.0 * y),
                    (2, -2.0 * z),
                    (3, jnp.ones_like(x)),
                    (5, square),
                    (6, -field_of(x, y, z)),
                ),
            )
            h, m, l = split3(block)
            features[i * 4 + q] = jnp.concatenate((h, h, h, m, m, l), axis=0).T.astype(BF16)
        return carry

    lax.fori_loop(0, features.shape[0] // 4, cell_chunk, 0)
    fetches[1].wait()

    def step(g, carry):
        near_group(g, pairs, stations, features, out, 0)
        return carry

    lax.fori_loop(0, jnp.minimum(near_groups(counts), HALF), step, 0)


def near_second_kernel(counts, pairs, stations, features, out):
    def step(g, carry):
        near_group(g, pairs, stations, features, out, HALF)
        return carry

    lax.fori_loop(HALF, near_groups(counts), step, 0)


def block_mask():
    lines = lax.broadcasted_iota(jnp.int32, (GROUP * VECS, TILE), 0) // VECS
    lanes = lax.broadcasted_iota(jnp.int32, (GROUP * VECS, TILE), 1) // (TILE // GROUP)
    return lines == lanes


def near_groups(counts):
    return counts[0, lax.axis_index("cel")] // GROUP


def contract(a, b, dim):
    return lax.dot_general(a, b, (((1,), (dim,)), ((), ())), preferred_element_type=F32)


def lanes_of(column):
    return pl.ds(pl.multiple_of(column * TILE, TILE), TILE)


def place(row):
    share = row >> 2
    return (share & (WIDE - 1)) * TALL + (share >> 3), lanes_of(row & 3)


def forward_kernel(counts, near, mid, *refs):
    parts = refs[:8]
    u_ref, v_ref, first_blocks, second_blocks, out, stacked, vectors, total = refs[8:]
    for k in range(8):
        stacked[2 * k : 2 * k + 2, :] = parts[k][...].astype(F32)
    vectors[...] = stacked[...].astype(BF16)
    total[...] = jnp.zeros_like(total)
    mask = block_mask()

    sums = []
    for g in range(u_ref.shape[0]):
        source = jnp.concatenate(
            [vectors[:, lanes_of(mid[1, g * GROUP + j])] for j in range(GROUP)], axis=0
        )
        reduced = contract(source, v_ref[g], 1)
        reduced = jnp.where(mask, reduced, 0.0).astype(BF16)
        sums.append(contract(reduced, u_ref[g], 0))
    for g in range(u_ref.shape[0]):
        for j in range(GROUP):
            slot, lanes = place(mid[0, g * GROUP + j])
            total[slot, :, lanes] += sums[g][j * VECS : (j + 1) * VECS]

    def near_step(g, carry, blocks, first):
        sums = [
            contract(vectors[:, lanes_of(near[1, g * GROUP + j])], blocks[(g - first) * GROUP + j], 0)
            for j in range(GROUP)
        ]
        for j in range(GROUP):
            slot, lanes = place(near[0, g * GROUP + j])
            total[slot, :, lanes] += sums[j]
        return carry

    groups = near_groups(counts)
    first_step = functools.partial(near_step, blocks=first_blocks, first=0)
    second_step = functools.partial(near_step, blocks=second_blocks, first=HALF)
    lax.fori_loop(0, jnp.minimum(groups, HALF), first_step, 0)
    lax.fori_loop(HALF, groups, second_step, 0)
    out[...] = total[...].astype(BF16)


def sum_of(parts):
    total = parts[0].astype(F32)
    for k in range(1, parts.shape[0]):
        total = total + parts[k].astype(F32)
    return total


def share_sum_kernel(parts, out):
    out[...] = sum_of(parts).astype(BF16)


def weigh_kernel(own, one, two, three, weights, predicted, weighted):
    sta, cel = lax.axis_index("sta"), lax.axis_index("cel")
    for h in range(TALL):
        total = own[h].astype(F32) + one[h].astype(F32)
        total = total + (two[h].astype(F32) + three[h].astype(F32))

        @pl.when(cel // WIDE == h)
        def _():
            for place_of in range(8):

                @pl.when(sta == place_of)
                def _():
                    for k in range(8):
                        line = 2 * (k ^ place_of)
                        predicted[line : line + 2, :] = total[2 * k : 2 * k + 2]

        share = h * WIDE + cel % WIDE
        scale = weights[pl.ds(pl.multiple_of(share * 8, 8), 8), :]
        for r in range(8):
            at = slice(r * 128, (r + 1) * 128)
            value = (total[:, at] * scale[r : r + 1, :]).astype(BF16)
            for i in range(WIDE):
                weighted[i, h, :, at] = value


def adjoint_kernel(
    counts, near, mid, data, u_ref, v_ref, first_blocks, second_blocks, kept, swapped, total
):
    total[...] = jnp.zeros_like(total)
    mask = block_mask()

    def station_tile(row):
        slot, lanes = place(row)
        return data[slot, :, lanes]

    sums = []
    for g in range(u_ref.shape[0]):
        source = jnp.concatenate(
            [station_tile(mid[0, g * GROUP + j]) for j in range(GROUP)], axis=0
        )
        pulled = contract(source, u_ref[g], 1)
        pulled = jnp.where(mask, pulled, 0.0).astype(BF16)
        sums.append(contract(pulled, v_ref[g], 0))
    for g in range(u_ref.shape[0]):
        for j in range(GROUP):
            lanes = lanes_of(mid[1, g * GROUP + j])
            total[:, lanes] += sums[g][j * VECS : (j + 1) * VECS]

    def near_step(g, carry, blocks, first):
        sums = [
            contract(station_tile(near[0, g * GROUP + j]), blocks[(g - first) * GROUP + j], 1)
            for j in range(GROUP)
        ]
        for j in range(GROUP):
            total[:, lanes_of(near[1, g * GROUP + j])] += sums[j]
        return carry

    groups = near_groups(counts)
    first_step = functools.partial(near_step, blocks=first_blocks, first=0)
    second_step = functools.partial(near_step, blocks=second_blocks, first=HALF)
    lax.fori_loop(0, jnp.minimum(groups, HALF), first_step, 0)
    lax.fori_loop(HALF, groups, second_step, 0)
    for t in range(4):
        kept[2 * t : 2 * t + 2, :] = total[4 * t : 4 * t + 2, :]
    swapped[...] = jnp.concatenate(
        [total[4 * t + 2 : 4 * t + 4, :] for t in range(4)], axis=0
    ).astype(BF16)


def chip_sum_kernel(kept, swapped, *outs):
    total = kept[...] + swapped[...].astype(F32)
    for t in range(4):
        outs[t][...] = total[2 * t : 2 * t + 2].astype(outs[t].dtype)


def params(mib):
    return pltpu.CompilerParams(vmem_limit_bytes=mib * MIB)


def body(
    model_vectors, station_xyz, cell_xyz, weights, near_pairs, near_count, mid_pairs, mid_u, mid_v
):
    slots = near_pairs.shape[2]
    near = near_pairs[0, 0].T
    mid = mid_pairs[0, 0].T
    u_factor = mid_u.reshape(-1, TILE, TILE)
    v_factor = mid_v.reshape(-1, TILE, TILE)

    def over_sta(x, k):
        return lax.ppermute(x, "sta", [(i, i ^ k) for i in range(8)])

    wide_groups = [[WIDE * h + w for w in range(WIDE)] for h in range(TALL)]

    def over_tall(x, k):
        return lax.ppermute(x, "cel", [(i, i ^ (WIDE * k)) for i in range(32)])

    def trade(x, axis, groups):
        return lax.all_to_all(x, axis, 0, 0, axis_index_groups=groups)

    half = HALF * GROUP
    cell_tiles = cell_xyz.shape[1] // TILE
    same_core = [over_sta(model_vectors, 2 * k) for k in range(1, 4)]
    inputs = (near_count, near, station_xyz, cell_xyz)
    first_blocks, features, stations = pl.pallas_call(
        near_first_kernel,
        in_specs=[SMEM] * 2 + [HBM] * 2,
        out_specs=[VMEM] * 3,
        out_shape=[
            jax.ShapeDtypeStruct((half, TILE, TILE), BF16),
            jax.ShapeDtypeStruct((cell_tiles, TILE, 48), BF16),
            jax.ShapeDtypeStruct(station_xyz.shape, F32),
        ],
        scratch_shapes=[pltpu.VMEM(cell_xyz.shape, F32), pltpu.SemaphoreType.DMA((2,))],
        compiler_params=params(16),
        cost_estimate=pl.CostEstimate(
            flops=half * 2 * 512 * 48 * 256, bytes_accessed=6 * MIB, transcendentals=half * 65536
        ),
        name="near_first",
    )(*[pltpu.with_memory_space_constraint(a, pltpu.HBM) for a in inputs])
    same_core, features = lax.optimization_barrier((same_core, features))
    vector_parts = []
    for vectors in [model_vectors] + same_core:
        vector_parts += [vectors, over_sta(vectors, 1)]
    second_blocks = pl.pallas_call(
        near_second_kernel,
        in_specs=[SMEM] * 2 + [VMEM] * 2,
        out_specs=VMEM,
        out_shape=jax.ShapeDtypeStruct((slots - half, TILE, TILE), BF16),
        compiler_params=params(16),
        cost_estimate=pl.CostEstimate(
            flops=half * 2 * 512 * 48 * 256, bytes_accessed=6 * MIB, transcendentals=half * 65536
        ),
        name="near_second",
    )(near_count, near, stations, features)

    wide = jax.ShapeDtypeStruct((WIDE, TALL, VECS, 1024), BF16)
    tall = jax.ShapeDtypeStruct((TALL, VECS, 1024), BF16)
    shares = pl.pallas_call(
        forward_kernel,
        in_specs=[SMEM] * 3 + [VMEM] * 12,
        out_specs=VMEM,
        out_shape=jax.ShapeDtypeStruct((32, VECS, 1024), BF16),
        scratch_shapes=[
            pltpu.VMEM((VECS, 8192), F32),
            pltpu.VMEM((VECS, 8192), BF16),
            pltpu.VMEM((32, VECS, 1024), F32),
        ],
        compiler_params=params(24),
        name="forward",
    )(near_count, near, mid, *vector_parts, u_factor, v_factor, first_blocks, second_blocks)

    sums = pl.pallas_call(
        share_sum_kernel,
        in_specs=[VMEM],
        out_specs=VMEM,
        out_shape=tall,
        compiler_params=params(8),
        name="share_sum",
    )(trade(shares.reshape(wide.shape), "cel", wide_groups))
    predicted, weighted = pl.pallas_call(
        weigh_kernel,
        in_specs=[VMEM] * 5,
        out_specs=[VMEM] * 2,
        out_shape=[jax.ShapeDtypeStruct((VECS, 1024), F32), wide],
        compiler_params=params(8),
        name="weigh",
    )(sums, *[over_tall(sums, k) for k in range(1, TALL)], weights.reshape(-1, 128))
    data = trade(weighted, "cel", wide_groups).reshape(32, VECS, 1024)

    lines = jax.ShapeDtypeStruct((8, 8192), BF16)
    kept, swapped = pl.pallas_call(
        adjoint_kernel,
        in_specs=[SMEM] * 3 + [VMEM] * 5,
        out_specs=[VMEM] * 2,
        out_shape=[jax.ShapeDtypeStruct(lines.shape, F32), lines],
        scratch_shapes=[pltpu.VMEM((VECS, 8192), F32)],
        compiler_params=params(24),
        name="adjoint",
    )(near_count, near, mid, data, u_factor, v_factor, first_blocks, second_blocks)
    pair = jax.ShapeDtypeStruct((2, 8192), BF16)
    terms = pl.pallas_call(
        chip_sum_kernel,
        in_specs=[VMEM] * 2,
        out_specs=[VMEM] * 4,
        out_shape=[jax.ShapeDtypeStruct(pair.shape, F32)] + [pair] * 3,
        compiler_params=params(4),
        name="chip_sum",
    )(kept, over_sta(swapped, 1))
    gradient = terms[0]
    for t in range(1, 4):
        gradient = gradient + over_sta(terms[t], 2 * t).astype(F32)
    return (predicted, gradient)


def solution(mesh):
    return jax.shard_map(
        body,
        mesh=mesh,
        in_specs=(
            P("sta", "cel"),
            P(None, "sta"),
            P(None, "cel"),
            P("sta"),
            P("sta", "cel", None, None),
            P("sta", None),
            P("sta", "cel", None, None),
            P("sta", "cel", None, None, None),
            P("sta", "cel", None, None, None),
        ),
        out_specs=(P(None, ("sta", "cel")), P("sta", "cel")),
        check_vma=False,
    )
```

```python
import functools

import jax
import jax.numpy as jnp
from jax import lax
from jax.experimental import pallas as pl
from jax.experimental.pallas import tpu as pltpu
from jax.sharding import PartitionSpec as P

VOLUME = 0.03125
FIELD = (0.17101, 0.46985, -0.86603)
SHRINK = VOLUME ** (-1.0 / 3.0)
SLOPE = 3.0**0.5

TILE = 256
VECS = 16
GROUP = 8
MIB = 1 << 20
WIDE = 8
TALL = 4
HALF = 4
BATCH = 4
F32 = jnp.float32
BF16 = jnp.bfloat16

SMEM = pl.BlockSpec(memory_space=pltpu.SMEM)
VMEM = pl.BlockSpec(memory_space=pltpu.VMEM)
HBM = pl.BlockSpec(memory_space=pltpu.HBM)


def split3(x):
    high = x.astype(BF16).astype(F32)
    rest = x - high
    middle = rest.astype(BF16).astype(F32)
    return high, middle, rest - middle


def stack(lines, values):
    total = jnp.zeros(lines.shape, F32)
    for line, value in values:
        total = jnp.where(lines == line, value, total)
    return total


def field_of(x, y, z):
    return SLOPE * (FIELD[0] * x + FIELD[1] * y + FIELD[2] * z)


def near_group(g, pairs, stations, features, out, first):
    lines = lax.broadcasted_iota(jnp.int32, (8, TILE), 0)
    for j in range(GROUP):
        at = lanes_of(pairs[0, g * GROUP + j])
        x, y, z = (SHRINK * stations[d : d + 1, at] for d in range(3))
        one = jnp.ones_like(x)
        wide = stack(lines, ((0, x), (1, y), (2, z), (3, x * x + y * y + z * z), (5, one)))
        flat = stack(lines, ((3, field_of(x, y, z)), (6, one)))
        left = features[pairs[1, g * GROUP + j]]

        def product(block):
            h, m, l = split3(block)
            right = jnp.concatenate((h, m, l, h, m, h), axis=0).astype(BF16)
            return jnp.dot(left, right, preferred_element_type=F32)

        inverse = lax.rsqrt(product(wide))
        along = product(flat)
        square = inverse * inverse
        along = along * square
        out[(g - first) * GROUP + j] = ((along * along - square) * inverse).astype(BF16)


def near_first_kernel(counts, pairs, station_hbm, cell_hbm, out, features, stations, cells, sem):
    fetches = [
        pltpu.make_async_copy(cell_hbm, cells, sem.at[0]),
        pltpu.make_async_copy(station_hbm, stations, sem.at[1]),
    ]
    for fetch in fetches:
        fetch.start()
    fetches[0].wait()

    def cell_chunk(i, carry):
        lines = lax.broadcasted_iota(jnp.int32, (8, TILE), 0)
        for q in range(4):
            at = lanes_of(i * 4 + q)
            x, y, z = (SHRINK * cells[d : d + 1, at] for d in range(3))
            square = x * x + y * y + z * z
            block = stack(
                lines,
                (
                    (0, -2.0 * x),
                    (1, -2.0 * y),
                    (2, -2.0 * z),
                    (3, jnp.ones_like(x)),
                    (5, square),
                    (6, -field_of(x, y, z)),
                ),
            )
            h, m, l = split3(block)
            features[i * 4 + q] = jnp.concatenate((h, h, h, m, m, l), axis=0).T.astype(BF16)
        return carry

    lax.fori_loop(0, features.shape[0] // 4, cell_chunk, 0)
    fetches[1].wait()

    def step(g, carry):
        near_group(g, pairs, stations, features, out, 0)
        return carry

    lax.fori_loop(0, jnp.minimum(near_groups(counts), HALF), step, 0)


def near_second_kernel(counts, pairs, stations, features, out):
    def step(g, carry):
        near_group(g, pairs, stations, features, out, HALF)
        return carry

    lax.fori_loop(HALF, near_groups(counts), step, 0)


def block_mask():
    lines = lax.broadcasted_iota(jnp.int32, (GROUP * VECS, TILE), 0) // VECS
    lanes = lax.broadcasted_iota(jnp.int32, (GROUP * VECS, TILE), 1) // (TILE // GROUP)
    return lines == lanes


def near_groups(counts):
    return counts[0, lax.axis_index("cel")] // GROUP


def contract(a, b, dim):
    return lax.dot_general(a, b, (((1,), (dim,)), ((), ())), preferred_element_type=F32)


def lanes_of(column):
    return pl.ds(pl.multiple_of(column * TILE, TILE), TILE)


def place(row):
    share = row >> 2
    return (share & (WIDE - 1)) * TALL + (share >> 3), lanes_of(row & 3)


def forward_kernel(counts, near, mid, *refs):
    parts = refs[:8]
    u_ref, v_ref, first_blocks, second_blocks, out, stacked, vectors, total = refs[8:]
    for k in range(8):
        stacked[2 * k : 2 * k + 2, :] = parts[k][...].astype(F32)
    vectors[...] = stacked[...].astype(BF16)
    total[...] = jnp.zeros_like(total)
    mask = block_mask()

    for start in range(0, u_ref.shape[0], BATCH):
        batch = range(start, start + BATCH)
        sources = [
            jnp.concatenate(
                [vectors[:, lanes_of(mid[1, g * GROUP + j])] for j in range(GROUP)], axis=0
            )
            for g in batch
        ]
        reduced = [contract(sources[g - start], v_ref[g], 1) for g in batch]
        reduced = [jnp.where(mask, x, 0.0).astype(BF16) for x in reduced]
        sums = [contract(reduced[g - start], u_ref[g], 0) for g in batch]
        for g in batch:
            for j in range(GROUP):
                slot, lanes = place(mid[0, g * GROUP + j])
                total[slot, :, lanes] += sums[g - start][j * VECS : (j + 1) * VECS]

    def near_step(g, carry, blocks, first):
        sums = [
            contract(vectors[:, lanes_of(near[1, g * GROUP + j])], blocks[(g - first) * GROUP + j], 0)
            for j in range(GROUP)
        ]
        for j in range(GROUP):
            slot, lanes = place(near[0, g * GROUP + j])
            total[slot, :, lanes] += sums[j]
        return carry

    groups = near_groups(counts)
    first_step = functools.partial(near_step, blocks=first_blocks, first=0)
    second_step = functools.partial(near_step, blocks=second_blocks, first=HALF)
    lax.fori_loop(0, jnp.minimum(groups, HALF), first_step, 0)
    lax.fori_loop(HALF, groups, second_step, 0)
    out[...] = total[...].astype(BF16)


def sum_of(parts):
    total = parts[0].astype(F32)
    for k in range(1, parts.shape[0]):
        total = total + parts[k].astype(F32)
    return total


def share_sum_kernel(parts, out):
    out[...] = sum_of(parts).astype(BF16)


def weigh_kernel(own, one, two, three, weights, predicted, weighted):
    sta, cel = lax.axis_index("sta"), lax.axis_index("cel")
    for h in range(TALL):
        total = own[h].astype(F32) + one[h].astype(F32)
        total = total + (two[h].astype(F32) + three[h].astype(F32))

        @pl.when(cel // WIDE == h)
        def _():
            for place_of in range(8):

                @pl.when(sta == place_of)
                def _():
                    for k in range(8):
                        line = 2 * (k ^ place_of)
                        predicted[line : line + 2, :] = total[2 * k : 2 * k + 2]

        share = h * WIDE + cel % WIDE
        scale = weights[pl.ds(pl.multiple_of(share * 8, 8), 8), :]
        for r in range(8):
            at = slice(r * 128, (r + 1) * 128)
            value = (total[:, at] * scale[r : r + 1, :]).astype(BF16)
            for i in range(WIDE):
                weighted[i, h, :, at] = value


def adjoint_kernel(
    counts, near, mid, data, u_ref, v_ref, first_blocks, second_blocks, kept, swapped, total
):
    total[...] = jnp.zeros_like(total)
    mask = block_mask()

    def station_tile(row):
        slot, lanes = place(row)
        return data[slot, :, lanes]

    for start in range(0, u_ref.shape[0], BATCH):
        batch = range(start, start + BATCH)
        sources = [
            jnp.concatenate(
                [station_tile(mid[0, g * GROUP + j]) for j in range(GROUP)], axis=0
            )
            for g in batch
        ]
        pulled = [contract(sources[g - start], u_ref[g], 1) for g in batch]
        pulled = [jnp.where(mask, x, 0.0).astype(BF16) for x in pulled]
        sums = [contract(pulled[g - start], v_ref[g], 0) for g in batch]
        for g in batch:
            for j in range(GROUP):
                lanes = lanes_of(mid[1, g * GROUP + j])
                total[:, lanes] += sums[g - start][j * VECS : (j + 1) * VECS]

    def near_step(g, carry, blocks, first):
        sums = [
            contract(station_tile(near[0, g * GROUP + j]), blocks[(g - first) * GROUP + j], 1)
            for j in range(GROUP)
        ]
        for j in range(GROUP):
            total[:, lanes_of(near[1, g * GROUP + j])] += sums[j]
        return carry

    groups = near_groups(counts)
    first_step = functools.partial(near_step, blocks=first_blocks, first=0)
    second_step = functools.partial(near_step, blocks=second_blocks, first=HALF)
    lax.fori_loop(0, jnp.minimum(groups, HALF), first_step, 0)
    lax.fori_loop(HALF, groups, second_step, 0)
    for t in range(4):
        kept[2 * t : 2 * t + 2, :] = total[4 * t : 4 * t + 2, :]
    swapped[...] = jnp.concatenate(
        [total[4 * t + 2 : 4 * t + 4, :] for t in range(4)], axis=0
    ).astype(BF16)


def chip_sum_kernel(kept, swapped, *outs):
    total = kept[...] + swapped[...].astype(F32)
    for t in range(4):
        outs[t][...] = total[2 * t : 2 * t + 2].astype(outs[t].dtype)


def params(mib):
    return pltpu.CompilerParams(vmem_limit_bytes=mib * MIB)


def body(
    model_vectors, station_xyz, cell_xyz, weights, near_pairs, near_count, mid_pairs, mid_u, mid_v
):
    slots = near_pairs.shape[2]
    near = near_pairs[0, 0].T
    mid = mid_pairs[0, 0].T
    u_factor = mid_u.reshape(-1, TILE, TILE)
    v_factor = mid_v.reshape(-1, TILE, TILE)

    def over_sta(x, k):
        return lax.ppermute(x, "sta", [(i, i ^ k) for i in range(8)])

    wide_groups = [[WIDE * h + w for w in range(WIDE)] for h in range(TALL)]

    def over_tall(x, k):
        return lax.ppermute(x, "cel", [(i, i ^ (WIDE * k)) for i in range(32)])

    def trade(x, axis, groups):
        return lax.all_to_all(x, axis, 0, 0, axis_index_groups=groups)

    half = HALF * GROUP
    cell_tiles = cell_xyz.shape[1] // TILE
    same_core = [over_sta(model_vectors, 2 * k) for k in range(1, 4)]
    inputs = (near_count, near, station_xyz, cell_xyz)
    first_blocks, features, stations = pl.pallas_call(
        near_first_kernel,
        in_specs=[SMEM] * 2 + [HBM] * 2,
        out_specs=[VMEM] * 3,
        out_shape=[
            jax.ShapeDtypeStruct((half, TILE, TILE), BF16),
            jax.ShapeDtypeStruct((cell_tiles, TILE, 48), BF16),
            jax.ShapeDtypeStruct(station_xyz.shape, F32),
        ],
        scratch_shapes=[pltpu.VMEM(cell_xyz.shape, F32), pltpu.SemaphoreType.DMA((2,))],
        compiler_params=params(16),
        cost_estimate=pl.CostEstimate(
            flops=half * 2 * 512 * 48 * 256, bytes_accessed=6 * MIB, transcendentals=half * 65536
        ),
        name="near_first",
    )(*[pltpu.with_memory_space_constraint(a, pltpu.HBM) for a in inputs])
    same_core, features = lax.optimization_barrier((same_core, features))
    vector_parts = []
    for vectors in [model_vectors] + same_core:
        vector_parts += [vectors, over_sta(vectors, 1)]
    second_blocks = pl.pallas_call(
        near_second_kernel,
        in_specs=[SMEM] * 2 + [VMEM] * 2,
        out_specs=VMEM,
        out_shape=jax.ShapeDtypeStruct((slots - half, TILE, TILE), BF16),
        compiler_params=params(16),
        cost_estimate=pl.CostEstimate(
            flops=half * 2 * 512 * 48 * 256, bytes_accessed=6 * MIB, transcendentals=half * 65536
        ),
        name="near_second",
    )(near_count, near, stations, features)

    wide = jax.ShapeDtypeStruct((WIDE, TALL, VECS, 1024), BF16)
    tall = jax.ShapeDtypeStruct((TALL, VECS, 1024), BF16)
    shares = pl.pallas_call(
        forward_kernel,
        in_specs=[SMEM] * 3 + [VMEM] * 12,
        out_specs=VMEM,
        out_shape=jax.ShapeDtypeStruct((32, VECS, 1024), BF16),
        scratch_shapes=[
            pltpu.VMEM((VECS, 8192), F32),
            pltpu.VMEM((VECS, 8192), BF16),
            pltpu.VMEM((32, VECS, 1024), F32),
        ],
        compiler_params=params(24),
        name="forward",
    )(near_count, near, mid, *vector_parts, u_factor, v_factor, first_blocks, second_blocks)

    sums = pl.pallas_call(
        share_sum_kernel,
        in_specs=[VMEM],
        out_specs=VMEM,
        out_shape=tall,
        compiler_params=params(8),
        name="share_sum",
    )(trade(shares.reshape(wide.shape), "cel", wide_groups))
    predicted, weighted = pl.pallas_call(
        weigh_kernel,
        in_specs=[VMEM] * 5,
        out_specs=[VMEM] * 2,
        out_shape=[jax.ShapeDtypeStruct((VECS, 1024), F32), wide],
        compiler_params=params(8),
        name="weigh",
    )(sums, *[over_tall(sums, k) for k in range(1, TALL)], weights.reshape(-1, 128))
    data = trade(weighted, "cel", wide_groups).reshape(32, VECS, 1024)

    lines = jax.ShapeDtypeStruct((8, 8192), BF16)
    kept, swapped = pl.pallas_call(
        adjoint_kernel,
        in_specs=[SMEM] * 3 + [VMEM] * 5,
        out_specs=[VMEM] * 2,
        out_shape=[jax.ShapeDtypeStruct(lines.shape, F32), lines],
        scratch_shapes=[pltpu.VMEM((VECS, 8192), F32)],
        compiler_params=params(24),
        name="adjoint",
    )(near_count, near, mid, data, u_factor, v_factor, first_blocks, second_blocks)
    pair = jax.ShapeDtypeStruct((2, 8192), BF16)
    terms = pl.pallas_call(
        chip_sum_kernel,
        in_specs=[VMEM] * 2,
        out_specs=[VMEM] * 4,
        out_shape=[jax.ShapeDtypeStruct(pair.shape, F32)] + [pair] * 3,
        compiler_params=params(4),
        name="chip_sum",
    )(kept, over_sta(swapped, 1))
    gradient = terms[0]
    for t in range(1, 4):
        gradient = gradient + over_sta(terms[t], 2 * t).astype(F32)
    return (predicted, gradient)


def solution(mesh):
    return jax.shard_map(
        body,
        mesh=mesh,
        in_specs=(
            P("sta", "cel"),
            P(None, "sta"),
            P(None, "cel"),
            P("sta"),
            P("sta", "cel", None, None),
            P("sta", None),
            P("sta", "cel", None, None),
            P("sta", "cel", None, None, None),
            P("sta", "cel", None, None, None),
        ),
        out_specs=(P(None, ("sta", "cel")), P("sta", "cel")),
        check_vma=False,
    )
```

```python
import functools

import jax
import jax.numpy as jnp
from jax import lax
from jax.experimental import pallas as pl
from jax.experimental.pallas import tpu as pltpu
from jax.sharding import PartitionSpec as P

VOLUME = 0.03125
FIELD = (0.17101, 0.46985, -0.86603)
SHRINK = VOLUME ** (-1.0 / 3.0)
SLOPE = 3.0**0.5

TILE = 256
VECS = 16
GROUP = 8
MIB = 1 << 20
WIDE = 8
TALL = 4
HALF = 4
BATCH = 4
F32 = jnp.float32
BF16 = jnp.bfloat16

SMEM = pl.BlockSpec(memory_space=pltpu.SMEM)
VMEM = pl.BlockSpec(memory_space=pltpu.VMEM)
HBM = pl.BlockSpec(memory_space=pltpu.HBM)


def split3(x):
    high = x.astype(BF16).astype(F32)
    rest = x - high
    middle = rest.astype(BF16).astype(F32)
    return high, middle, rest - middle


def stack(lines, values):
    total = jnp.zeros(lines.shape, F32)
    for line, value in values:
        total = jnp.where(lines == line, value, total)
    return total


def field_of(x, y, z):
    return SLOPE * (FIELD[0] * x + FIELD[1] * y + FIELD[2] * z)


def near_group(g, pairs, stations, features, out, first):
    lines = lax.broadcasted_iota(jnp.int32, (8, TILE), 0)
    for j in range(GROUP):
        at = lanes_of(pairs[0, g * GROUP + j])
        x, y, z = (SHRINK * stations[d : d + 1, at] for d in range(3))
        one = jnp.ones_like(x)
        wide = stack(lines, ((0, x), (1, y), (2, z), (3, x * x + y * y + z * z), (5, one)))
        flat = stack(lines, ((3, field_of(x, y, z)), (6, one)))
        left = features[pairs[1, g * GROUP + j]]

        def product(block):
            h, m, l = split3(block)
            right = jnp.concatenate((h, m, l, h, m, h), axis=0).astype(BF16)
            return jnp.dot(left, right, preferred_element_type=F32)

        inverse = lax.rsqrt(product(wide))
        along = product(flat)
        square = inverse * inverse
        along = along * square
        out[(g - first) * GROUP + j] = ((along * along - square) * inverse).astype(BF16)


def near_first_kernel(counts, pairs, station_hbm, cell_hbm, out, features, stations, cells, sem):
    fetches = [
        pltpu.make_async_copy(cell_hbm, cells, sem.at[0]),
        pltpu.make_async_copy(station_hbm, stations, sem.at[1]),
    ]
    for fetch in fetches:
        fetch.start()
    fetches[0].wait()

    def cell_chunk(i, carry):
        lines = lax.broadcasted_iota(jnp.int32, (8, TILE), 0)
        for q in range(4):
            at = lanes_of(i * 4 + q)
            x, y, z = (SHRINK * cells[d : d + 1, at] for d in range(3))
            square = x * x + y * y + z * z
            block = stack(
                lines,
                (
                    (0, -2.0 * x),
                    (1, -2.0 * y),
                    (2, -2.0 * z),
                    (3, jnp.ones_like(x)),
                    (5, square),
                    (6, -field_of(x, y, z)),
                ),
            )
            h, m, l = split3(block)
            features[i * 4 + q] = jnp.concatenate((h, h, h, m, m, l), axis=0).T.astype(BF16)
        return carry

    lax.fori_loop(0, features.shape[0] // 4, cell_chunk, 0)
    fetches[1].wait()

    def step(g, carry):
        near_group(g, pairs, stations, features, out, 0)
        return carry

    lax.fori_loop(0, jnp.minimum(near_groups(counts), HALF), step, 0)


def near_second_kernel(counts, pairs, stations, features, out):
    def step(g, carry):
        near_group(g, pairs, stations, features, out, HALF)
        return carry

    lax.fori_loop(HALF, near_groups(counts), step, 0)


def block_mask():
    lines = lax.broadcasted_iota(jnp.int32, (GROUP * VECS, TILE), 0) // VECS
    lanes = lax.broadcasted_iota(jnp.int32, (GROUP * VECS, TILE), 1) // (TILE // GROUP)
    return lines == lanes


def near_groups(counts):
    return counts[0, lax.axis_index("cel")] // GROUP


def contract(a, b, dim):
    return lax.dot_general(a, b, (((1,), (dim,)), ((), ())), preferred_element_type=F32)


def lanes_of(column):
    return pl.ds(pl.multiple_of(column * TILE, TILE), TILE)


def place(row):
    share = row >> 2
    return (share & (WIDE - 1)) * TALL + (share >> 3), lanes_of(row & 3)


def forward_kernel(counts, near, mid, *refs):
    parts = refs[:8]
    u_ref, v_ref, first_blocks, second_blocks, out, stacked, vectors, total = refs[8:]
    for k in range(8):
        stacked[2 * k : 2 * k + 2, :] = parts[k][...].astype(F32)
    vectors[...] = stacked[...].astype(BF16)
    total[...] = jnp.zeros_like(total)
    mask = block_mask()

    for start in range(0, u_ref.shape[0], BATCH):
        batch = range(start, start + BATCH)
        sources = [
            jnp.concatenate(
                [vectors[:, lanes_of(mid[1, g * GROUP + j])] for j in range(GROUP)], axis=0
            )
            for g in batch
        ]
        reduced = [contract(sources[g - start], v_ref[g], 1) for g in batch]
        reduced = [jnp.where(mask, x, 0.0).astype(BF16) for x in reduced]
        sums = [contract(reduced[g - start], u_ref[g], 0) for g in batch]
        for g in batch:
            for j in range(GROUP):
                slot, lanes = place(mid[0, g * GROUP + j])
                total[slot, :, lanes] += sums[g - start][j * VECS : (j + 1) * VECS]

    def near_step(g, carry, blocks, first):
        sums = [
            contract(vectors[:, lanes_of(near[1, g * GROUP + j])], blocks[(g - first) * GROUP + j], 0)
            for j in range(GROUP)
        ]
        for j in range(GROUP):
            slot, lanes = place(near[0, g * GROUP + j])
            total[slot, :, lanes] += sums[j]
        return carry

    groups = near_groups(counts)
    first_step = functools.partial(near_step, blocks=first_blocks, first=0)
    second_step = functools.partial(near_step, blocks=second_blocks, first=HALF)
    lax.fori_loop(0, jnp.minimum(groups, HALF), first_step, 0)
    lax.fori_loop(HALF, groups, second_step, 0)
    out[...] = total[...].astype(BF16)


def share_sum_kernel(parts, *outs):
    row = lax.axis_index("cel") // WIDE
    for k in range(TALL):
        total = parts[0, row ^ k].astype(F32)
        for w in range(1, WIDE):
            total = total + parts[w, row ^ k].astype(F32)
        outs[k][...] = total.astype(outs[k].dtype)


def weigh_kernel(own, one, two, three, weights, predicted, weighted):
    sta, cel = lax.axis_index("sta"), lax.axis_index("cel")
    total = own[...] + one[...].astype(F32) + two[...].astype(F32) + three[...].astype(F32)
    scale = weights[pl.ds(pl.multiple_of(cel * 8, 8), 8), :]
    for r in range(8):
        at = slice(r * 128, (r + 1) * 128)
        weighted[:, at] = (total[:, at] * scale[r : r + 1, :]).astype(BF16)
    for place_of in range(8):

        @pl.when(sta == place_of)
        def _():
            for k in range(8):
                line = 2 * (k ^ place_of)
                predicted[line : line + 2, :] = total[2 * k : 2 * k + 2]


def copies_kernel(*refs):
    columns, out = refs[:TALL], refs[TALL]
    row = lax.axis_index("cel") // WIDE
    for k in range(TALL):
        value = columns[k][...]
        for w in range(WIDE):
            out[w, row ^ k] = value


def adjoint_kernel(
    counts, near, mid, data, u_ref, v_ref, first_blocks, second_blocks, kept, swapped, total
):
    total[...] = jnp.zeros_like(total)
    mask = block_mask()

    def station_tile(row):
        slot, lanes = place(row)
        return data[slot, :, lanes]

    for start in range(0, u_ref.shape[0], BATCH):
        batch = range(start, start + BATCH)
        sources = [
            jnp.concatenate(
                [station_tile(mid[0, g * GROUP + j]) for j in range(GROUP)], axis=0
            )
            for g in batch
        ]
        pulled = [contract(sources[g - start], u_ref[g], 1) for g in batch]
        pulled = [jnp.where(mask, x, 0.0).astype(BF16) for x in pulled]
        sums = [contract(pulled[g - start], v_ref[g], 0) for g in batch]
        for g in batch:
            for j in range(GROUP):
                lanes = lanes_of(mid[1, g * GROUP + j])
                total[:, lanes] += sums[g - start][j * VECS : (j + 1) * VECS]

    def near_step(g, carry, blocks, first):
        sums = [
            contract(station_tile(near[0, g * GROUP + j]), blocks[(g - first) * GROUP + j], 1)
            for j in range(GROUP)
        ]
        for j in range(GROUP):
            total[:, lanes_of(near[1, g * GROUP + j])] += sums[j]
        return carry

    groups = near_groups(counts)
    first_step = functools.partial(near_step, blocks=first_blocks, first=0)
    second_step = functools.partial(near_step, blocks=second_blocks, first=HALF)
    lax.fori_loop(0, jnp.minimum(groups, HALF), first_step, 0)
    lax.fori_loop(HALF, groups, second_step, 0)
    for t in range(4):
        kept[2 * t : 2 * t + 2, :] = total[4 * t : 4 * t + 2, :]
    swapped[...] = jnp.concatenate(
        [total[4 * t + 2 : 4 * t + 4, :] for t in range(4)], axis=0
    ).astype(BF16)


def chip_sum_kernel(kept, swapped, *outs):
    total = kept[...] + swapped[...].astype(F32)
    for t in range(4):
        outs[t][...] = total[2 * t : 2 * t + 2].astype(outs[t].dtype)


def params(mib):
    return pltpu.CompilerParams(vmem_limit_bytes=mib * MIB)


def body(
    model_vectors, station_xyz, cell_xyz, weights, near_pairs, near_count, mid_pairs, mid_u, mid_v
):
    slots = near_pairs.shape[2]
    near = near_pairs[0, 0].T
    mid = mid_pairs[0, 0].T
    u_factor = mid_u.reshape(-1, TILE, TILE)
    v_factor = mid_v.reshape(-1, TILE, TILE)

    def over_sta(x, k):
        return lax.ppermute(x, "sta", [(i, i ^ k) for i in range(8)])

    wide_groups = [[WIDE * h + w for w in range(WIDE)] for h in range(TALL)]

    def over_tall(x, k):
        return lax.ppermute(x, "cel", [(i, i ^ (WIDE * k)) for i in range(32)])

    def trade(x, axis, groups):
        return lax.all_to_all(x, axis, 0, 0, axis_index_groups=groups)

    half = HALF * GROUP
    cell_tiles = cell_xyz.shape[1] // TILE
    same_core = [over_sta(model_vectors, 2 * k) for k in range(1, 4)]
    inputs = (near_count, near, station_xyz, cell_xyz)
    first_blocks, features, stations = pl.pallas_call(
        near_first_kernel,
        in_specs=[SMEM] * 2 + [HBM] * 2,
        out_specs=[VMEM] * 3,
        out_shape=[
            jax.ShapeDtypeStruct((half, TILE, TILE), BF16),
            jax.ShapeDtypeStruct((cell_tiles, TILE, 48), BF16),
            jax.ShapeDtypeStruct(station_xyz.shape, F32),
        ],
        scratch_shapes=[pltpu.VMEM(cell_xyz.shape, F32), pltpu.SemaphoreType.DMA((2,))],
        compiler_params=params(16),
        cost_estimate=pl.CostEstimate(
            flops=half * 2 * 512 * 48 * 256, bytes_accessed=6 * MIB, transcendentals=half * 65536
        ),
        name="near_first",
    )(*[pltpu.with_memory_space_constraint(a, pltpu.HBM) for a in inputs])
    same_core, features = lax.optimization_barrier((same_core, features))
    vector_parts = []
    for vectors in [model_vectors] + same_core:
        vector_parts += [vectors, over_sta(vectors, 1)]
    second_blocks = pl.pallas_call(
        near_second_kernel,
        in_specs=[SMEM] * 2 + [VMEM] * 2,
        out_specs=VMEM,
        out_shape=jax.ShapeDtypeStruct((slots - half, TILE, TILE), BF16),
        compiler_params=params(16),
        cost_estimate=pl.CostEstimate(
            flops=half * 2 * 512 * 48 * 256, bytes_accessed=6 * MIB, transcendentals=half * 65536
        ),
        name="near_second",
    )(near_count, near, stations, features)

    wide = jax.ShapeDtypeStruct((WIDE, TALL, VECS, 1024), BF16)
    shares = pl.pallas_call(
        forward_kernel,
        in_specs=[SMEM] * 3 + [VMEM] * 12,
        out_specs=VMEM,
        out_shape=jax.ShapeDtypeStruct((32, VECS, 1024), BF16),
        scratch_shapes=[
            pltpu.VMEM((VECS, 8192), F32),
            pltpu.VMEM((VECS, 8192), BF16),
            pltpu.VMEM((32, VECS, 1024), F32),
        ],
        compiler_params=params(24),
        name="forward",
    )(near_count, near, mid, *vector_parts, u_factor, v_factor, first_blocks, second_blocks)

    narrow = jax.ShapeDtypeStruct((VECS, 1024), BF16)
    full = jax.ShapeDtypeStruct((VECS, 1024), F32)
    sums = pl.pallas_call(
        share_sum_kernel,
        in_specs=[VMEM],
        out_specs=[VMEM] * TALL,
        out_shape=[full] + [narrow] * (TALL - 1),
        compiler_params=params(8),
        name="share_sum",
    )(trade(shares.reshape(wide.shape), "cel", wide_groups))
    predicted, weighted = pl.pallas_call(
        weigh_kernel,
        in_specs=[VMEM] * 5,
        out_specs=[VMEM] * 2,
        out_shape=[full, narrow],
        compiler_params=params(8),
        name="weigh",
    )(sums[0], *[over_tall(sums[k], k) for k in range(1, TALL)], weights.reshape(-1, 128))
    copies = pl.pallas_call(
        copies_kernel,
        in_specs=[VMEM] * TALL,
        out_specs=VMEM,
        out_shape=wide,
        compiler_params=params(8),
        name="copies",
    )(weighted, *[over_tall(weighted, k) for k in range(1, TALL)])
    data = trade(copies, "cel", wide_groups).reshape(32, VECS, 1024)

    lines = jax.ShapeDtypeStruct((8, 8192), BF16)
    kept, swapped = pl.pallas_call(
        adjoint_kernel,
        in_specs=[SMEM] * 3 + [VMEM] * 5,
        out_specs=[VMEM] * 2,
        out_shape=[jax.ShapeDtypeStruct(lines.shape, F32), lines],
        scratch_shapes=[pltpu.VMEM((VECS, 8192), F32)],
        compiler_params=params(24),
        name="adjoint",
    )(near_count, near, mid, data, u_factor, v_factor, first_blocks, second_blocks)
    pair = jax.ShapeDtypeStruct((2, 8192), BF16)
    terms = pl.pallas_call(
        chip_sum_kernel,
        in_specs=[VMEM] * 2,
        out_specs=[VMEM] * 4,
        out_shape=[jax.ShapeDtypeStruct(pair.shape, F32)] + [pair] * 3,
        compiler_params=params(4),
        name="chip_sum",
    )(kept, over_sta(swapped, 1))
    gradient = terms[0]
    for t in range(1, 4):
        gradient = gradient + over_sta(terms[t], 2 * t).astype(F32)
    return (predicted, gradient)


def solution(mesh):
    return jax.shard_map(
        body,
        mesh=mesh,
        in_specs=(
            P("sta", "cel"),
            P(None, "sta"),
            P(None, "cel"),
            P("sta"),
            P("sta", "cel", None, None),
            P("sta", None),
            P("sta", "cel", None, None),
            P("sta", "cel", None, None, None),
            P("sta", "cel", None, None, None),
        ),
        out_specs=(P(None, ("sta", "cel")), P("sta", "cel")),
        check_vma=False,
    )
```

```python
import functools

import jax
import jax.numpy as jnp
from jax import lax
from jax.experimental import pallas as pl
from jax.experimental.pallas import tpu as pltpu
from jax.sharding import PartitionSpec as P

VOLUME = 0.03125
FIELD = (0.17101, 0.46985, -0.86603)
SHRINK = VOLUME ** (-1.0 / 3.0)
SLOPE = 3.0**0.5

TILE = 256
VECS = 16
GROUP = 8
MIB = 1 << 20
WIDE = 8
TALL = 4
HALF = 4
BATCH = 4
F32 = jnp.float32
BF16 = jnp.bfloat16

SMEM = pl.BlockSpec(memory_space=pltpu.SMEM)
VMEM = pl.BlockSpec(memory_space=pltpu.VMEM)
HBM = pl.BlockSpec(memory_space=pltpu.HBM)


def split3(x):
    high = x.astype(BF16).astype(F32)
    rest = x - high
    middle = rest.astype(BF16).astype(F32)
    return high, middle, rest - middle


def stack(lines, values):
    total = jnp.zeros(lines.shape, F32)
    for line, value in values:
        total = jnp.where(lines == line, value, total)
    return total


def field_of(x, y, z):
    return SLOPE * (FIELD[0] * x + FIELD[1] * y + FIELD[2] * z)


def near_group(g, pairs, stations, features, out, first):
    lines = lax.broadcasted_iota(jnp.int32, (8, TILE), 0)
    for j in range(GROUP):
        at = lanes_of(pairs[0, g * GROUP + j])
        x, y, z = (SHRINK * stations[d : d + 1, at] for d in range(3))
        one = jnp.ones_like(x)
        wide = stack(lines, ((0, x), (1, y), (2, z), (3, x * x + y * y + z * z), (5, one)))
        flat = stack(lines, ((3, field_of(x, y, z)), (6, one)))
        left = features[pairs[1, g * GROUP + j]]

        def product(block):
            h, m, l = split3(block)
            right = jnp.concatenate((h, m, l, h, m, h), axis=0).astype(BF16)
            return jnp.dot(left, right, preferred_element_type=F32)

        inverse = lax.rsqrt(product(wide))
        along = product(flat)
        square = inverse * inverse
        along = along * square
        out[(g - first) * GROUP + j] = ((along * along - square) * inverse).astype(BF16)


def near_first_kernel(counts, pairs, station_hbm, cell_hbm, out, features, stations, cells, sem):
    fetches = [
        pltpu.make_async_copy(cell_hbm, cells, sem.at[0]),
        pltpu.make_async_copy(station_hbm, stations, sem.at[1]),
    ]
    for fetch in fetches:
        fetch.start()
    fetches[0].wait()

    def cell_chunk(i, carry):
        lines = lax.broadcasted_iota(jnp.int32, (8, TILE), 0)
        for q in range(8):
            at = lanes_of(i * 8 + q)
            x, y, z = (SHRINK * cells[d : d + 1, at] for d in range(3))
            square = x * x + y * y + z * z
            block = stack(
                lines,
                (
                    (0, -2.0 * x),
                    (1, -2.0 * y),
                    (2, -2.0 * z),
                    (3, jnp.ones_like(x)),
                    (5, square),
                    (6, -field_of(x, y, z)),
                ),
            )
            h, m, l = split3(block)
            features[i * 8 + q] = jnp.concatenate((h, h, h, m, m, l), axis=0).T.astype(BF16)
        return carry

    lax.fori_loop(0, features.shape[0] // 8, cell_chunk, 0)
    fetches[1].wait()

    def step(g, carry):
        near_group(g, pairs, stations, features, out, 0)
        return carry

    lax.fori_loop(0, jnp.minimum(near_groups(counts), HALF), step, 0)


def near_second_kernel(counts, pairs, stations, features, out):
    def step(g, carry):
        near_group(g, pairs, stations, features, out, HALF)
        return carry

    lax.fori_loop(HALF, near_groups(counts), step, 0)


def block_mask():
    lines = lax.broadcasted_iota(jnp.int32, (GROUP * VECS, TILE), 0) // VECS
    lanes = lax.broadcasted_iota(jnp.int32, (GROUP * VECS, TILE), 1) // (TILE // GROUP)
    return lines == lanes


def near_groups(counts):
    return counts[0, lax.axis_index("cel")] // GROUP


def contract(a, b, dim):
    return lax.dot_general(a, b, (((1,), (dim,)), ((), ())), preferred_element_type=F32)


def lanes_of(column):
    return pl.ds(pl.multiple_of(column * TILE, TILE), TILE)


def place(row):
    share = row >> 2
    return (share & (WIDE - 1)) * TALL + (share >> 3), lanes_of(row & 3)


def forward_kernel(counts, near, mid, *refs):
    parts = refs[:8]
    u_ref, v_ref, first_blocks, second_blocks, out, stacked, vectors, total = refs[8:]
    for k in range(8):
        stacked[2 * k : 2 * k + 2, :] = parts[k][...].astype(F32)
    vectors[...] = stacked[...].astype(BF16)
    total[...] = jnp.zeros_like(total)
    mask = block_mask()

    for start in range(0, u_ref.shape[0], BATCH):
        batch = range(start, start + BATCH)
        sources = [
            jnp.concatenate(
                [vectors[:, lanes_of(mid[1, g * GROUP + j])] for j in range(GROUP)], axis=0
            )
            for g in batch
        ]
        reduced = [contract(sources[g - start], v_ref[g], 1) for g in batch]
        reduced = [jnp.where(mask, x, 0.0).astype(BF16) for x in reduced]
        sums = [contract(reduced[g - start], u_ref[g], 0) for g in batch]
        for g in batch:
            for j in range(GROUP):
                slot, lanes = place(mid[0, g * GROUP + j])
                total[slot, :, lanes] += sums[g - start][j * VECS : (j + 1) * VECS]

    def near_step(g, carry, blocks, first):
        sums = [
            contract(vectors[:, lanes_of(near[1, g * GROUP + j])], blocks[(g - first) * GROUP + j], 0)
            for j in range(GROUP)
        ]
        for j in range(GROUP):
            slot, lanes = place(near[0, g * GROUP + j])
            total[slot, :, lanes] += sums[j]
        return carry

    groups = near_groups(counts)
    first_step = functools.partial(near_step, blocks=first_blocks, first=0)
    second_step = functools.partial(near_step, blocks=second_blocks, first=HALF)
    lax.fori_loop(0, jnp.minimum(groups, HALF), first_step, 0)
    lax.fori_loop(HALF, groups, second_step, 0)
    out[...] = total[...].astype(BF16)


def sum_of(parts):
    total = parts[0].astype(F32)
    for k in range(1, parts.shape[0]):
        total = total + parts[k].astype(F32)
    return total


def share_sum_kernel(parts, out):
    out[...] = sum_of(parts).astype(BF16)


def weigh_kernel(own, one, two, three, weights, predicted, weighted):
    sta, cel = lax.axis_index("sta"), lax.axis_index("cel")
    for h in range(TALL):
        total = own[h].astype(F32) + one[h].astype(F32)
        total = total + (two[h].astype(F32) + three[h].astype(F32))

        @pl.when(cel // WIDE == h)
        def _():
            for place_of in range(8):

                @pl.when(sta == place_of)
                def _():
                    for k in range(8):
                        line = 2 * (k ^ place_of)
                        predicted[line : line + 2, :] = total[2 * k : 2 * k + 2]

        share = h * WIDE + cel % WIDE
        scale = weights[pl.ds(pl.multiple_of(share * 8, 8), 8), :]
        for r in range(8):
            at = slice(r * 128, (r + 1) * 128)
            value = (total[:, at] * scale[r : r + 1, :]).astype(BF16)
            for i in range(WIDE):
                weighted[i, h, :, at] = value


def adjoint_kernel(
    counts, near, mid, data, u_ref, v_ref, first_blocks, second_blocks, kept, swapped, total
):
    total[...] = jnp.zeros_like(total)
    mask = block_mask()

    def station_tile(row):
        slot, lanes = place(row)
        return data[slot, :, lanes]

    for start in range(0, u_ref.shape[0], BATCH):
        batch = range(start, start + BATCH)
        sources = [
            jnp.concatenate(
                [station_tile(mid[0, g * GROUP + j]) for j in range(GROUP)], axis=0
            )
            for g in batch
        ]
        pulled = [contract(sources[g - start], u_ref[g], 1) for g in batch]
        pulled = [jnp.where(mask, x, 0.0).astype(BF16) for x in pulled]
        sums = [contract(pulled[g - start], v_ref[g], 0) for g in batch]
        for g in batch:
            for j in range(GROUP):
                lanes = lanes_of(mid[1, g * GROUP + j])
                total[:, lanes] += sums[g - start][j * VECS : (j + 1) * VECS]

    def near_step(g, carry, blocks, first):
        sums = [
            contract(station_tile(near[0, g * GROUP + j]), blocks[(g - first) * GROUP + j], 1)
            for j in range(GROUP)
        ]
        for j in range(GROUP):
            total[:, lanes_of(near[1, g * GROUP + j])] += sums[j]
        return carry

    groups = near_groups(counts)
    first_step = functools.partial(near_step, blocks=first_blocks, first=0)
    second_step = functools.partial(near_step, blocks=second_blocks, first=HALF)
    lax.fori_loop(0, jnp.minimum(groups, HALF), first_step, 0)
    lax.fori_loop(HALF, groups, second_step, 0)
    for t in range(4):
        kept[2 * t : 2 * t + 2, :] = total[4 * t : 4 * t + 2, :]
    swapped[...] = jnp.concatenate(
        [total[4 * t + 2 : 4 * t + 4, :] for t in range(4)], axis=0
    ).astype(BF16)


def chip_sum_kernel(kept, swapped, *outs):
    total = kept[...] + swapped[...].astype(F32)
    for t in range(4):
        outs[t][...] = total[2 * t : 2 * t + 2].astype(outs[t].dtype)


def params(mib):
    return pltpu.CompilerParams(vmem_limit_bytes=mib * MIB)


def body(
    model_vectors, station_xyz, cell_xyz, weights, near_pairs, near_count, mid_pairs, mid_u, mid_v
):
    slots = near_pairs.shape[2]
    near = near_pairs[0, 0].T
    mid = mid_pairs[0, 0].T
    u_factor = mid_u.reshape(-1, TILE, TILE)
    v_factor = mid_v.reshape(-1, TILE, TILE)

    def over_sta(x, k):
        return lax.ppermute(x, "sta", [(i, i ^ k) for i in range(8)])

    wide_groups = [[WIDE * h + w for w in range(WIDE)] for h in range(TALL)]

    def over_tall(x, k):
        return lax.ppermute(x, "cel", [(i, i ^ (WIDE * k)) for i in range(32)])

    def trade(x, axis, groups):
        return lax.all_to_all(x, axis, 0, 0, axis_index_groups=groups)

    half = HALF * GROUP
    cell_tiles = cell_xyz.shape[1] // TILE
    same_core = [over_sta(model_vectors, 2 * k) for k in range(1, 4)]
    inputs = (near_count, near, station_xyz, cell_xyz)
    first_blocks, features, stations = pl.pallas_call(
        near_first_kernel,
        in_specs=[SMEM] * 2 + [HBM] * 2,
        out_specs=[VMEM] * 3,
        out_shape=[
            jax.ShapeDtypeStruct((half, TILE, TILE), BF16),
            jax.ShapeDtypeStruct((cell_tiles, TILE, 48), BF16),
            jax.ShapeDtypeStruct(station_xyz.shape, F32),
        ],
        scratch_shapes=[pltpu.VMEM(cell_xyz.shape, F32), pltpu.SemaphoreType.DMA((2,))],
        compiler_params=params(16),
        cost_estimate=pl.CostEstimate(
            flops=half * 2 * 512 * 48 * 256, bytes_accessed=6 * MIB, transcendentals=half * 65536
        ),
        name="near_first",
    )(*[pltpu.with_memory_space_constraint(a, pltpu.HBM) for a in inputs])
    same_core, features = lax.optimization_barrier((same_core, features))
    vector_parts = []
    for vectors in [model_vectors] + same_core:
        vector_parts += [vectors, over_sta(vectors, 1)]
    second_blocks = pl.pallas_call(
        near_second_kernel,
        in_specs=[SMEM] * 2 + [VMEM] * 2,
        out_specs=VMEM,
        out_shape=jax.ShapeDtypeStruct((slots - half, TILE, TILE), BF16),
        compiler_params=params(16),
        cost_estimate=pl.CostEstimate(
            flops=half * 2 * 512 * 48 * 256, bytes_accessed=6 * MIB, transcendentals=half * 65536
        ),
        name="near_second",
    )(near_count, near, stations, features)

    wide = jax.ShapeDtypeStruct((WIDE, TALL, VECS, 1024), BF16)
    tall = jax.ShapeDtypeStruct((TALL, VECS, 1024), BF16)
    shares = pl.pallas_call(
        forward_kernel,
        in_specs=[SMEM] * 3 + [VMEM] * 12,
        out_specs=VMEM,
        out_shape=jax.ShapeDtypeStruct((32, VECS, 1024), BF16),
        scratch_shapes=[
            pltpu.VMEM((VECS, 8192), F32),
            pltpu.VMEM((VECS, 8192), BF16),
            pltpu.VMEM((32, VECS, 1024), F32),
        ],
        compiler_params=params(24),
        name="forward",
    )(near_count, near, mid, *vector_parts, u_factor, v_factor, first_blocks, second_blocks)

    sums = pl.pallas_call(
        share_sum_kernel,
        in_specs=[VMEM],
        out_specs=VMEM,
        out_shape=tall,
        compiler_params=params(8),
        name="share_sum",
    )(trade(shares.reshape(wide.shape), "cel", wide_groups))
    predicted, weighted = pl.pallas_call(
        weigh_kernel,
        in_specs=[VMEM] * 5,
        out_specs=[VMEM] * 2,
        out_shape=[jax.ShapeDtypeStruct((VECS, 1024), F32), wide],
        compiler_params=params(8),
        name="weigh",
    )(sums, *[over_tall(sums, k) for k in range(1, TALL)], weights.reshape(-1, 128))
    data = trade(weighted, "cel", wide_groups).reshape(32, VECS, 1024)

    lines = jax.ShapeDtypeStruct((8, 8192), BF16)
    kept, swapped = pl.pallas_call(
        adjoint_kernel,
        in_specs=[SMEM] * 3 + [VMEM] * 5,
        out_specs=[VMEM] * 2,
        out_shape=[jax.ShapeDtypeStruct(lines.shape, F32), lines],
        scratch_shapes=[pltpu.VMEM((VECS, 8192), F32)],
        compiler_params=params(24),
        name="adjoint",
    )(near_count, near, mid, data, u_factor, v_factor, first_blocks, second_blocks)
    pair = jax.ShapeDtypeStruct((2, 8192), BF16)
    terms = pl.pallas_call(
        chip_sum_kernel,
        in_specs=[VMEM] * 2,
        out_specs=[VMEM] * 4,
        out_shape=[jax.ShapeDtypeStruct(pair.shape, F32)] + [pair] * 3,
        compiler_params=params(4),
        name="chip_sum",
    )(kept, over_sta(swapped, 1))
    gradient = terms[0]
    for t in range(1, 4):
        gradient = gradient + over_sta(terms[t], 2 * t).astype(F32)
    return (predicted, gradient)


def solution(mesh):
    return jax.shard_map(
        body,
        mesh=mesh,
        in_specs=(
            P("sta", "cel"),
            P(None, "sta"),
            P(None, "cel"),
            P("sta"),
            P("sta", "cel", None, None),
            P("sta", None),
            P("sta", "cel", None, None),
            P("sta", "cel", None, None, None),
            P("sta", "cel", None, None, None),
        ),
        out_specs=(P(None, ("sta", "cel")), P("sta", "cel")),
        check_vma=False,
    )
```
